32 devices in a mesh: row: 4 (over x, core), col: 8 (over z, y).
Axes of the slice: x: 2, y: 2, z: 4, core: 2. Of those that a mesh axis runs over, the one named last changes fastest.
Arguments:
- observations: float32 [1024, 8192], P('row', 'col'), may hold values from -6 to 6
- omega: float32 [8, 3, 16, 128, 128], P('col'), as said below
- block_slots: int32 [8, 3, 16], P('col'), may hold values from -1 to 63, as said below
Outputs:
- new_omega: float32 [8, 3, 16, 128, 128], P('col', None, 'row')
The draws below stay inside these ranges and needn't reach their ends.
Inputs may be any that keep to these rules, and one draw needn't show every extreme that they name: `block_slots`: active slots come first in each tile. The pattern is symmetric: slot j of [t, 2] and slot j of [t + 1, 0] (modulo 8) name mirrored blocks, a and b swapped; in [t, 1] the 8 diagonal blocks come first in order, then mirrored pairs side by side. Some tile has all 16 slots active. `omega`: the blocks of active slots form one symmetric matrix: the block of slot j of [t, 2] is the transpose of that of slot j of [t + 1, 0], mirrored pairs of [t, 1] are transposes of each other, and diagonal blocks are symmetric with diagonal entries of 0.8 or more. Empty slots hold arbitrary values.
All inputs are finite; a program needn't handle non-finite values.
Results may differ from the reference program's by a relative error of at most 0.0003.
Values sent between devices are 32-bit elements; how exact they have to be, the bound alone decides.
A program may use at most 128 MiB of HBM per device.

```python
import jax
import jax.numpy as jnp
import numpy as np
from jax import lax

TILE = 1024
BLK = 128
KMAX = 16
SAMPLES = 1024
VARS = 8192
N_COL = 8


def slot_layout(key):
    tile_blocks = TILE // BLK
    capacity = min(KMAX, tile_blocks * tile_blocks)
    pair_most = (capacity - tile_blocks) // 2
    keys_all = jax.random.split(jax.random.fold_in(key, 11), 6)
    strips = jnp.arange(N_COL)
    counts = jax.random.randint(keys_all[0], (N_COL,), 1, capacity + 1)
    chosen = jax.random.randint(keys_all[1], (), 0, N_COL)
    counts = jnp.where(strips == chosen, capacity, counts)
    orders = jax.vmap(lambda sub_key: jax.random.permutation(sub_key, tile_blocks * tile_blocks))(jax.random.split(keys_all[2], N_COL))
    upper = orders[:, :capacity].astype(jnp.int32)
    upper = jnp.where(jnp.arange(capacity)[None, :] < counts[:, None], upper, -1)
    upper = jnp.pad(upper, ((0, 0), (0, KMAX - capacity)), constant_values=-1)
    mirrored = jnp.where(upper >= 0, upper % tile_blocks * tile_blocks + upper // tile_blocks, -1)
    lower = jnp.roll(mirrored, 1, axis=0)
    rows_table, cols_table = np.triu_indices(tile_blocks, 1)
    rows_jnp = jnp.asarray(rows_table, jnp.int32)
    cols_jnp = jnp.asarray(cols_table, jnp.int32)
    pair_orders = jax.vmap(lambda sub_key: jax.random.permutation(sub_key, rows_table.size))(jax.random.split(keys_all[3], N_COL))[:, :pair_most]
    first_pos = rows_jnp[pair_orders] * tile_blocks + cols_jnp[pair_orders]
    second_pos = cols_jnp[pair_orders] * tile_blocks + rows_jnp[pair_orders]
    pair_counts = jax.random.randint(keys_all[4], (N_COL,), 0, pair_most + 1)
    chosen_pair = jax.random.randint(keys_all[5], (), 0, N_COL)
    pair_counts = jnp.where(strips == chosen_pair, pair_most, pair_counts)
    live_pairs = jnp.arange(pair_most)[None, :] < pair_counts[:, None]
    first_pos = jnp.where(live_pairs, first_pos, -1)
    second_pos = jnp.where(live_pairs, second_pos, -1)
    pairs = jnp.stack([first_pos, second_pos], axis=2).reshape(N_COL, 2 * pair_most).astype(jnp.int32)
    diagonal = jnp.broadcast_to(jnp.arange(tile_blocks, dtype=jnp.int32) * (tile_blocks + 1), (N_COL, tile_blocks))
    centre = jnp.concatenate([diagonal, pairs], axis=1)
    centre = jnp.pad(centre, ((0, 0), (0, KMAX - tile_blocks - 2 * pair_most)), constant_values=-1)
    return jnp.stack([lower, centre, upper], axis=1).astype(jnp.int32)


def draw_block_slots(key, part):
    return slot_layout(key)


def draw_omega(key, part):
    tile_blocks = TILE // BLK
    capacity = min(KMAX, tile_blocks * tile_blocks)
    pair_most = (capacity - tile_blocks) // 2
    keys_all = jax.random.split(jax.random.fold_in(key, 23), 3)
    shape = (N_COL, KMAX, BLK, BLK)
    upper = 0.1 * jax.random.normal(keys_all[0], shape, jnp.float32)
    raw_blocks = 0.1 * jax.random.normal(keys_all[1], shape, jnp.float32)
    diag_vals = jax.random.uniform(keys_all[2], (N_COL, KMAX, BLK), jnp.float32, 1.0, 2.0)
    lower = jnp.roll(jnp.swapaxes(upper, 2, 3), 1, axis=0)
    identity = jnp.eye(BLK, dtype=bool)
    symmetric = (raw_blocks + jnp.swapaxes(raw_blocks, 2, 3)) * 0.7071
    symmetric = jnp.where(identity, diag_vals[:, :, :, None], symmetric)
    source = np.arange(KMAX)
    second = np.zeros(KMAX, dtype=bool)
    for slot_index in range(tile_blocks, tile_blocks + 2 * pair_most):
        source[slot_index] = tile_blocks + 2 * ((slot_index - tile_blocks) // 2)
        second[slot_index] = (slot_index - tile_blocks) % 2 == 1
    paired = raw_blocks[:, source]
    paired = jnp.where(second[None, :, None, None], jnp.swapaxes(paired, 2, 3), paired)
    centre = jnp.where((np.arange(KMAX) < tile_blocks)[None, :, None, None], symmetric, paired)
    return jnp.stack([lower, centre, upper], axis=1)


def shard_levels(stream_key, shape, cuts, least, top_value):
    level, own = 1.0, jax.random.fold_in(stream_key, 6)
    for axis_at, parts in cuts:
        heights = jnp.exp(jax.random.uniform(jax.random.fold_in(own, axis_at), (parts,), jnp.float32, least / len(cuts), top_value / len(cuts)))
        level = level * jnp.repeat(heights, shape[axis_at] // parts).reshape([-1 if axis == axis_at else 1 for axis in range(len(shape))])
    return level


def gaussian(own_key, extent, width, most, pieces=(), kind=jnp.bfloat16):
    gain = shard_levels(own_key, extent, pieces, -0.22, 0.18) if pieces else 1.0
    entries = jax.random.normal(own_key, extent, jnp.float32) * width * gain
    return jnp.minimum(jnp.maximum(entries, -most), most).astype(kind)


def setup_inputs(seed: int = 0) -> dict:
    seeds = jax.random.split(jax.random.key(seed), 4)
    return {
        "observations": gaussian(seeds[0], (SAMPLES, VARS), 1.0, 6.0, ((0, 4), (1, 8)), jnp.float32),
        "omega": draw_omega(jax.random.fold_in(seeds[3], 71), 0),
        "block_slots": draw_block_slots(jax.random.fold_in(seeds[3], 71), 0),
    }


step_size = 0.5
penalty = 0.1
highest = lax.Precision.HIGHEST


def strip_terms(tile_view, omega_strip, slot_ids, column):
    tile_blocks = TILE // BLK
    nearby = jnp.stack([lax.dynamic_index_in_dim(tile_view, ((column + tile_step) % N_COL).astype(jnp.int32), 1, keepdims=False) for tile_step in (-1, 0, 1)])
    active = slot_ids >= 0
    row_pick = jax.nn.one_hot(jnp.where(active, slot_ids // tile_blocks, -1), tile_blocks, dtype=jnp.float32)
    col_pick = jax.nn.one_hot(jnp.where(active, slot_ids % tile_blocks, -1), tile_blocks, dtype=jnp.float32)
    chosen = jnp.einsum('ejn,epnk->ejpk', row_pick, nearby, precision=highest)
    product = jnp.einsum('ejpk,ejkl->ejpl', chosen, omega_strip, precision=highest)
    residual = jnp.einsum('ejn,ejpl->pnl', col_pick, product, precision=highest)
    picked = jnp.einsum('ejn,pnl->ejpl', col_pick, residual, precision=highest)
    return jnp.einsum('ejpk,ejpl->ejkl', chosen, picked, precision=highest)


def mirror_inner(forward_centre, centre_ids):
    tile_blocks = TILE // BLK
    active = centre_ids >= 0
    flipped = jnp.where(active, (centre_ids % tile_blocks) * tile_blocks + centre_ids // tile_blocks, -2)
    match_table = ((centre_ids[..., None, :] == flipped[..., :, None]) & active[..., None, :]).astype(jnp.float32)
    return jnp.einsum('...jk,...kab->...jba', match_table, forward_centre, precision=highest)


def proximal(omega_part, slot_part, smooth):
    tile_blocks = TILE // BLK
    active = slot_part >= 0
    centre_mask = (jnp.arange(3) == 1)[:, None]
    diagonal_block = active & centre_mask & (slot_part // tile_blocks == slot_part % tile_blocks)
    identity = jnp.eye(BLK, dtype=jnp.float32)
    own_diag = jnp.diagonal(omega_part, axis1=-2, axis2=-1)
    safe_diag = jnp.where(diagonal_block[..., None], own_diag, 1.0)
    inverse = jnp.where(diagonal_block[..., None], 1.0 / safe_diag, 0.0)
    gradient = smooth - inverse[..., None] * identity
    trial_step = omega_part - step_size * gradient
    shrunk = jnp.sign(trial_step) * jnp.maximum(jnp.abs(trial_step) - step_size * penalty, 0.0)
    keep_mask = diagonal_block[..., None, None] & (identity > 0.5)
    result = jnp.where(keep_mask, trial_step, shrunk)
    return jnp.where(active[..., None, None], result, 0.0)


def reference(observations, omega, block_slots):
    tile_blocks = TILE // BLK
    tile_view = observations.reshape(observations.shape[0], N_COL, tile_blocks, BLK)
    columns = jnp.arange(N_COL, dtype=jnp.int32)
    forward = lax.map(lambda strip_item: strip_terms(tile_view, strip_item[0], strip_item[1], strip_item[2]), (omega, block_slots, columns))
    forward = forward / SAMPLES
    from_below = jnp.swapaxes(jnp.roll(forward[:, 2], 1, axis=0), -1, -2)
    from_above = jnp.swapaxes(jnp.roll(forward[:, 0], -1, axis=0), -1, -2)
    inner_mirror = mirror_inner(forward[:, 1], block_slots[:, 1])
    mirror = jnp.stack([from_below, inner_mirror, from_above], axis=1)
    smooth = 0.5 * (forward + mirror)
    return proximal(omega, block_slots, smooth)
```

```python
import functools

import jax
import jax.numpy as jnp
from jax import lax
from jax.experimental import pallas as pl
from jax.experimental.pallas import tpu as pltpu
from jax.sharding import PartitionSpec as P

MESH = pl.DeviceIdType.MESH
BLK = 128
TB = 8
HALF = 128
CHUNKS = 8

step_size = 0.5
penalty = 0.1
f32, bf16 = jnp.float32, jnp.bfloat16


def split(value):
    high = value.astype(bf16)
    return high, (value - high.astype(f32)).astype(bf16)


def flip(index, mask):
    out, bit = index, 1
    while bit <= mask:
        if mask & bit:
            out = out + bit * (1 - 2 * lax.rem(lax.div(index, bit), 2))
        bit *= 2
    return out


def kernel(
    nr, nc, kmax, tab, obs, omega, out, near, far, xs, xt, wcat, cum, rs, fbuf, rbuf, mrecv,
    near_send, near_recv, far_send, far_recv, row_send, row_recv, mir_send, mir_recv,
):
    samples = obs.shape[0]
    share = kmax // nr
    bits = nr.bit_length() - 1
    r, c = lax.axis_index("row"), lax.axis_index("col")
    odd = lax.rem(c, 2)
    near_col = c + 1 - 2 * odd
    far_col = lax.rem(c - 1 + 2 * odd + nc, nc)
    relay_to = lax.rem(c + 2 - 4 * odd + nc, nc)
    relay_from = lax.rem(c - 2 + 4 * odd + nc, nc)
    strip = (1, 2 - 2 * odd, 2 * odd)

    barrier = pltpu.get_barrier_semaphore()
    partners = [{"col": near_col}, {"col": far_col}, {"col": relay_from}]
    partners += [{"row": flip(r, 1 << k)} for k in range(bits)]
    for partner in partners:
        pl.semaphore_signal(barrier, inc=1, device_id=partner, device_id_type=MESH)
    pl.semaphore_wait(barrier, len(partners))

    piece = samples // CHUNKS

    def near_copy(k):
        rows = pl.ds(k * piece, piece)
        return pltpu.make_async_remote_copy(
            obs.at[rows], near.at[rows], near_send.at[k], near_recv.at[k],
            device_id={"col": near_col}, device_id_type=MESH,
        )

    def far_copy(k):
        rows = pl.ds(k * piece, piece)
        return pltpu.make_async_remote_copy(
            near.at[rows], far.at[rows], far_send.at[k], far_recv.at[k],
            device_id={"col": relay_to}, device_id_type=MESH,
        )

    near_copies = [near_copy(k) for k in range(CHUNKS)]
    far_copies = [far_copy(k) for k in range(CHUNKS)]
    for copy in near_copies:
        copy.start()

    def relay(k):
        near_copies[k].wait_recv()
        far_copies[k].start()

    def convert(source, kind, h):
        rows = pl.ds(h * HALF, HALF)
        for a in range(TB):
            block = source[rows, pl.ds(a * BLK, BLK)]
            high, low = split(block)
            xs[kind * TB + a, rows, :] = jnp.concatenate([high, low], axis=1)
            high, low = split(block.T)
            xt[kind * TB + a, :, rows] = jnp.concatenate([high, low], axis=0)

    def entry(kind, at):
        return tab[strip[kind], at]

    def weights(kind):
        def body(at, _):
            slot = entry(kind, at)
            live = entry(kind, 2 * kmax + slot) >= 0
            high, low = split(jnp.where(live, omega[0, strip[kind], slot], 0.0))
            top = jnp.concatenate([high, low], axis=1)
            bottom = jnp.concatenate([high, jnp.zeros_like(low)], axis=1)
            wcat[kind * kmax + at] = jnp.concatenate([top, bottom], axis=0)
            return 0

        lax.fori_loop(0, kmax, body, 0, unroll=2)
        cum[kind * (kmax + 1) + kmax] = jnp.zeros((samples, BLK), f32)

    def products(kind, h):
        rows = pl.ds(h * HALF, HALF)

        def body(at, total):
            slot = entry(kind, at)
            keep = entry(kind, kmax + at).astype(f32)
            a = lax.div(jnp.maximum(entry(kind, 2 * kmax + slot), 0), TB)
            both = jnp.dot(
                xs[kind * TB + a, rows, :], wcat[kind * kmax + at], preferred_element_type=f32
            )
            total = total * keep + (both[:, :BLK] + both[:, BLK:])
            cum[kind * (kmax + 1) + at, rows, :] = total
            return total

        lax.fori_loop(0, kmax, body, jnp.zeros((HALF, BLK), f32), unroll=4)

    halves = samples // HALF
    per_half = CHUNKS // halves

    def own_work():
        for h in range(halves):
            yield lambda h=h: convert(obs, 0, h)
        yield lambda: weights(0)
        for h in range(halves):
            yield lambda h=h: products(0, h)
        yield lambda: weights(1)
        yield lambda: weights(2)

    for k, work in enumerate(own_work()):
        work()
        if k < CHUNKS:
            relay(k)
    done = min(k + 1, CHUNKS)
    for h in range(halves):
        while done < (h + 1) * per_half:
            relay(done)
            done += 1
        convert(near, 1, h)
        if done < CHUNKS:
            relay(done)
            done += 1
        products(1, h)
        for k in range(h * per_half, (h + 1) * per_half):
            far_copies[k].wait_recv()
        convert(far, 2, h)
        products(2, h)
    for copy in near_copies + far_copies:
        copy.wait_send()

    def collect(b, _):
        total = cum[entry(0, 3 * kmax + b)]
        for kind in (1, 2):
            total = total + cum[kind * (kmax + 1) + entry(kind, 3 * kmax + b)]
        high, low = split(total)
        rs[b] = jnp.concatenate([high, low], axis=1)
        return 0

    lax.fori_loop(0, TB, collect, 0, unroll=2)

    def forward(kind, slot):
        place = jnp.maximum(entry(kind, 2 * kmax + slot), 0)
        both = jnp.dot(
            xt[kind * TB + lax.div(place, TB)], rs[lax.rem(place, TB)], preferred_element_type=f32
        )
        both = both[:BLK] + both[BLK:]
        return both[:, :BLK] + both[:, BLK:]

    def mate(slot):
        return slot + lax.div(slot, TB) * (1 - 2 * lax.rem(slot, 2))

    paired_here = share % 2 == 0

    def row_copy(kind, q):
        bit = q & -q
        return pltpu.make_async_remote_copy(
            fbuf.at[kind, q], rbuf.at[kind, q - 1], row_send.at[kind, q - 1],
            row_recv.at[kind, q - 1], device_id={"row": flip(r, bit)}, device_id_type=MESH,
        )

    row_copies = {(kind, q): row_copy(kind, q) for kind in range(3) for q in range(1, nr)}

    def group(kind, q):
        first = flip(r, q) * share

        def body(s, _):
            part = forward(kind, first + s)
            if kind == 0 and not paired_here:
                part = part + forward(kind, mate(first + s)).T
            fbuf[kind, q, s] = part
            return 0

        lax.fori_loop(0, share, body, 0, unroll=True)

    def add_arrived(kind, q, bit):
        row_copies[kind, q | bit].wait_recv()
        fbuf[kind, q] = fbuf[kind, q] + rbuf[kind, (q | bit) - 1]

    def reduce(kind, q):
        group(kind, q)
        low = q & -q if q else nr // 2
        bit = 1
        while bit < low:
            add_arrived(kind, q, bit)
            bit *= 2
        if q:
            row_copies[kind, q].start()

    order = (1, 2, 0)
    for kind in order:
        for q in range(nr - 1, nr // 2 - 1, -1):
            reduce(kind, q)
    for kind in order:
        for q in range(nr // 2 - 1, -1, -1):
            reduce(kind, q)

    mirrors = {
        kind: pltpu.make_async_remote_copy(
            fbuf.at[kind, 0], mrecv.at[kind - 1], mir_send.at[kind - 1], mir_recv.at[kind - 1],
            device_id={"col": near_col if kind == 1 else far_col}, device_id_type=MESH,
        )
        for kind in (1, 2)
    }
    scale = 0.5 / (samples * nr)
    eye = lax.broadcasted_iota(jnp.int32, (BLK, BLK), 0) == lax.broadcasted_iota(jnp.int32, (BLK, BLK), 1)

    def finish(kind, s, mirrored):
        slot = r * share + s
        place = entry(kind, 2 * kmax + slot)
        gradient = fbuf[kind, 0, s] * scale if mirrored is None else (fbuf[kind, 0, s] + mirrored) * scale
        old = omega[0, strip[kind], slot]
        edge = step_size * penalty
        if kind == 0:
            on_diagonal = eye & (lax.div(place, TB) == lax.rem(place, TB)) & (place >= 0)
            inverse = jnp.where(on_diagonal, 1.0 / jnp.where(on_diagonal, old, 1.0), 0.0)
            gradient = gradient - inverse
        trial = old - step_size * gradient
        shrunk = jnp.where(trial > edge, trial - edge, jnp.where(trial < -edge, trial + edge, 0.0))
        if kind == 0:
            shrunk = jnp.where(on_diagonal, trial, shrunk)
        out[0, strip[kind], s] = jnp.where(place >= 0, shrunk, 0.0)

    for kind in order:
        if nr > 1:
            add_arrived(kind, 0, nr // 2)
        if kind:
            mirrors[kind].start()
    for s in range(share):
        if paired_here:
            other = s + lax.div(r * share, TB) * (1 - 2 * (s % 2))
            finish(0, s, fbuf[0, 0, other].T)
        else:
            finish(0, s, None)
    for kind in (1, 2):
        mirrors[kind].wait_recv()
        for s in range(share):
            finish(kind, s, mrecv[kind - 1, s].T)
    for copy in row_copies.values():
        copy.wait_send()
    for copy in mirrors.values():
        copy.wait_send()


def tables(slots):
    kmax = slots.shape[1]
    column = jnp.where(slots >= 0, slots % TB, TB)
    index = jnp.arange(kmax, dtype=jnp.int32)
    mine, other = column[:, :, None], column[:, None, :]
    ahead = (other < mine) | ((other == mine) & (index[None, :] < index[:, None]))
    rank = jnp.sum(ahead.astype(jnp.int32), axis=2)
    at = (rank[:, None, :] == index[:, None]).astype(jnp.int32)
    order = jnp.sum(at * index, axis=2)
    before = jnp.sum(((other == mine) & (index[None, :] < index[:, None])).astype(jnp.int32), axis=2)
    keep = jnp.sum(at * (before > 0).astype(jnp.int32)[:, None, :], axis=2)
    wanted = jnp.arange(TB, dtype=jnp.int32)[None, :, None]
    upto = jnp.sum((column[:, None, :] <= wanted).astype(jnp.int32), axis=2)
    within = jnp.sum((column[:, None, :] == wanted).astype(jnp.int32), axis=2)
    last = jnp.where(within > 0, upto - 1, kmax)
    return jnp.concatenate([order, keep, slots, last], axis=1).astype(jnp.int32)


def solution(mesh):
    nr, nc = mesh.shape["row"], mesh.shape["col"]

    def on_device(observations, omega, block_slots):
        samples, width = observations.shape
        kmax = omega.shape[2]
        share = kmax // nr
        vmem = pl.BlockSpec(memory_space=pltpu.VMEM)
        dma = pltpu.SemaphoreType.DMA
        return pl.pallas_call(
            functools.partial(kernel, nr, nc, kmax),
            out_shape=jax.ShapeDtypeStruct((1, 3, share, BLK, BLK), f32),
            in_specs=[pl.BlockSpec(memory_space=pltpu.SMEM), vmem, vmem],
            out_specs=vmem,
            scratch_shapes=[
                pltpu.VMEM((samples, width), f32),
                pltpu.VMEM((samples, width), f32),
                pltpu.VMEM((3 * TB, samples, 2 * BLK), bf16),
                pltpu.VMEM((3 * TB, 2 * BLK, samples), bf16),
                pltpu.VMEM((3 * kmax, 2 * BLK, 2 * BLK), bf16),
                pltpu.VMEM((3 * (kmax + 1), samples, BLK), f32),
                pltpu.VMEM((TB, samples, 2 * BLK), bf16),
                pltpu.VMEM((3, nr, share, BLK, BLK), f32),
                pltpu.VMEM((3, nr - 1, share, BLK, BLK), f32),
                pltpu.VMEM((2, share, BLK, BLK), f32),
                dma((CHUNKS,)),
                dma((CHUNKS,)),
                dma((CHUNKS,)),
                dma((CHUNKS,)),
                dma((3, nr - 1)),
                dma((3, nr - 1)),
                dma((2,)),
                dma((2,)),
            ],
            compiler_params=pltpu.CompilerParams(
                collective_id=0, has_side_effects=True, vmem_limit_bytes=56 * 1024 * 1024
            ),
        )(tables(block_slots[0]), observations, omega)

    return jax.shard_map(
        on_device,
        mesh=mesh,
        in_specs=(P("row", "col"), P("col", None, None, None, None), P("col", None, None)),
        out_specs=P("col", None, "row", None, None),
        check_vma=False,
    )
```

```python
import functools

import jax
import jax.numpy as jnp
from jax import lax
from jax.experimental import pallas as pl
from jax.experimental.pallas import tpu as pltpu
from jax.sharding import PartitionSpec as P

MESH = pl.DeviceIdType.MESH
BLK = 128
TB = 8
CHUNKS = 16
WINDOW = 4

step_size = 0.5
penalty = 0.1
f32, bf16 = jnp.float32, jnp.bfloat16


def split(value):
    high = value.astype(bf16)
    return high, (value - high.astype(f32)).astype(bf16)


def flip(index, mask):
    out, bit = index, 1
    while bit <= mask:
        if mask & bit:
            out = out + bit * (1 - 2 * lax.rem(lax.div(index, bit), 2))
        bit *= 2
    return out


def kernel(
    nr, nc, kmax, slots, obs_in, omega_in, out, tab, obs, omega, near, far, xs, xt, wcat, cum, rs, fbuf, rbuf,
    mrecv, load, near_send, near_recv, far_send, far_recv, row_send, row_recv, mir_send, mir_recv,
):
    samples = obs_in.shape[0]
    load_obs = pltpu.make_async_copy(obs_in, obs, load.at[0])
    load_omega = pltpu.make_async_copy(omega_in, omega, load.at[1])
    share = kmax // nr
    bits = nr.bit_length() - 1
    r, c = lax.axis_index("row"), lax.axis_index("col")
    odd = lax.rem(c, 2)
    near_col = c + 1 - 2 * odd
    far_col = lax.rem(c - 1 + 2 * odd + nc, nc)
    relay_to = lax.rem(c + 2 - 4 * odd + nc, nc)
    relay_from = lax.rem(c - 2 + 4 * odd + nc, nc)
    strip = (1, 2 - 2 * odd, 2 * odd)

    barrier = pltpu.get_barrier_semaphore()
    partners = [{"col": near_col}, {"col": far_col}, {"col": relay_from}]
    partners += [{"row": flip(r, 1 << k)} for k in range(bits)]
    for partner in partners:
        pl.semaphore_signal(barrier, inc=1, device_id=partner, device_id_type=MESH)
    pl.semaphore_wait(barrier, len(partners))

    piece = samples // CHUNKS

    def near_copy(k):
        rows = pl.ds(k * piece, piece)
        return pltpu.make_async_remote_copy(
            obs_in.at[rows], near.at[rows], near_send.at[k], near_recv.at[k],
            device_id={"col": near_col}, device_id_type=MESH,
        )

    def far_copy(k):
        rows = pl.ds(k * piece, piece)
        return pltpu.make_async_remote_copy(
            near.at[rows], far.at[rows], far_send.at[k], far_recv.at[k],
            device_id={"col": relay_to}, device_id_type=MESH,
        )

    near_copies = [near_copy(k) for k in range(CHUNKS)]
    far_copies = [far_copy(k) for k in range(CHUNKS)]
    for copy in near_copies[:WINDOW]:
        copy.start()
    load_obs.start()
    load_omega.start()

    def relay(k):
        near_copies[k].wait_recv()
        far_copies[k].start()
        near_copies[k].wait_send()
        if k + WINDOW < CHUNKS:
            near_copies[k + WINDOW].start()

    def convert(source, kind, first, count):
        rows = pl.ds(first, count)
        for a in range(TB):
            block = source[rows, pl.ds(a * BLK, BLK)]
            high, low = split(block)
            xs[kind * TB + a, rows, :] = jnp.concatenate([high, low], axis=1)
            high, low = split(block.T)
            xt[kind * TB + a, :, rows] = jnp.concatenate([high, low], axis=0)

    def fill(e, _):
        places = [slots[e, 0, j] for j in range(kmax)]
        columns = [jnp.where(p >= 0, lax.rem(jnp.maximum(p, 0), TB), TB) for p in places]
        for j in range(kmax):
            before = jnp.int32(kmax)
            for i in range(j):
                before = jnp.where(columns[i] == columns[j], i, before)
            tab[e, j] = before
        for b in range(TB):
            last = jnp.int32(kmax)
            for j in range(kmax):
                last = jnp.where(columns[j] == b, j, last)
            tab[e, kmax + b] = last
        return 0

    def entry(kind, at):
        return tab[strip[kind], at]

    def position(kind, slot):
        return slots[strip[kind], 0, slot]

    def weights(kind):
        def body(slot, _):
            live = position(kind, slot) >= 0
            high, low = split(jnp.where(live, omega[0, strip[kind], slot], 0.0))
            top = jnp.concatenate([high, low], axis=1)
            bottom = jnp.concatenate([high, jnp.zeros_like(low)], axis=1)
            wcat[kind * kmax + slot] = jnp.concatenate([top, bottom], axis=0)
            return 0

        lax.fori_loop(0, kmax, body, 0, unroll=2)
        cum[kind * (kmax + 1) + kmax] = jnp.zeros((samples, BLK), f32)

    def products(kind, first, count):
        rows = pl.ds(first, count)

        def body(slot, _):
            a = lax.div(jnp.maximum(position(kind, slot), 0), TB)
            both = jnp.dot(
                xs[kind * TB + a, rows, :], wcat[kind * kmax + slot], preferred_element_type=f32
            )
            before = cum[kind * (kmax + 1) + entry(kind, slot), rows, :]
            cum[kind * (kmax + 1) + slot, rows, :] = before + (both[:, :BLK] + both[:, BLK:])
            return 0

        lax.fori_loop(0, kmax, body, 0, unroll=4)

    piece_rows = samples // CHUNKS
    half, quarter = samples // 2, samples // 4
    done = 0

    def relay_to_row(row):
        nonlocal done
        while done < row // piece_rows:
            relay(done)
            done += 1

    def relay_next():
        nonlocal done
        if done < CHUNKS:
            relay(done)
            done += 1

    lax.fori_loop(0, 3, fill, 0)
    load_obs.wait()
    convert(obs, 0, 0, half)
    relay_next()
    convert(obs, 0, half, half)
    relay_next()
    load_omega.wait()
    weights(0)
    relay_next()
    products(0, 0, half)
    relay_next()
    products(0, half, half)
    relay_next()
    weights(1)
    relay_next()
    weights(2)
    for first, count in ((0, half), (half, quarter), (half + quarter, quarter)):
        relay_to_row(first + count)
        convert(near, 1, first, count)
        relay_next()
        products(1, first, count)
        relay_next()
        for k in range(first // piece_rows, (first + count) // piece_rows):
            far_copies[k].wait_recv()
        convert(far, 2, first, count)
        relay_next()
        products(2, first, count)
    for copy in far_copies:
        copy.wait_send()

    def collect(b, _):
        total = cum[entry(0, kmax + b)]
        for kind in (1, 2):
            total = total + cum[kind * (kmax + 1) + entry(kind, kmax + b)]
        high, low = split(total)
        rs[b] = jnp.concatenate([high, low], axis=1)
        return 0

    lax.fori_loop(0, TB, collect, 0, unroll=2)

    def forward(kind, slot):
        place = jnp.maximum(position(kind, slot), 0)
        both = jnp.dot(
            xt[kind * TB + lax.div(place, TB)], rs[lax.rem(place, TB)], preferred_element_type=f32
        )
        both = both[:BLK] + both[BLK:]
        return both[:, :BLK] + both[:, BLK:]

    def mate(slot):
        return slot + lax.div(slot, TB) * (1 - 2 * lax.rem(slot, 2))

    paired_here = share % 2 == 0

    def row_copy(kind, q):
        bit = q & -q
        return pltpu.make_async_remote_copy(
            fbuf.at[kind, q], rbuf.at[kind, q - 1], row_send.at[kind, q - 1],
            row_recv.at[kind, q - 1], device_id={"row": flip(r, bit)}, device_id_type=MESH,
        )

    row_copies = {(kind, q): row_copy(kind, q) for kind in range(3) for q in range(1, nr)}

    def group(kind, q):
        first = flip(r, q) * share

        def body(s, _):
            part = forward(kind, first + s)
            if kind == 0 and not paired_here:
                part = part + forward(kind, mate(first + s)).T
            fbuf[kind, q, s] = part
            return 0

        lax.fori_loop(0, share, body, 0, unroll=True)

    def add_arrived(kind, q, bit):
        row_copies[kind, q | bit].wait_recv()
        fbuf[kind, q] = fbuf[kind, q] + rbuf[kind, (q | bit) - 1]

    def reduce(kind, q):
        group(kind, q)
        low = q & -q if q else nr // 2
        bit = 1
        while bit < low:
            add_arrived(kind, q, bit)
            bit *= 2
        if q:
            row_copies[kind, q].start()

    order = (2, 1, 0)
    for kind in order:
        for q in range(nr - 1, nr // 2 - 1, -1):
            reduce(kind, q)
    for kind in order:
        for q in range(nr // 2 - 1, -1, -1):
            reduce(kind, q)

    mirrors = {
        kind: pltpu.make_async_remote_copy(
            fbuf.at[kind, 0], mrecv.at[kind - 1], mir_send.at[kind - 1], mir_recv.at[kind - 1],
            device_id={"col": near_col if kind == 1 else far_col}, device_id_type=MESH,
        )
        for kind in (1, 2)
    }
    scale = 0.5 / (samples * nr)
    eye = lax.broadcasted_iota(jnp.int32, (BLK, BLK), 0) == lax.broadcasted_iota(jnp.int32, (BLK, BLK), 1)

    def finish(kind, s, mirrored):
        slot = r * share + s
        place = position(kind, slot)
        gradient = fbuf[kind, 0, s] * scale if mirrored is None else (fbuf[kind, 0, s] + mirrored) * scale
        old = omega[0, strip[kind], slot]
        edge = step_size * penalty
        if kind == 0:
            on_diagonal = eye & (lax.div(place, TB) == lax.rem(place, TB)) & (place >= 0)
            inverse = jnp.where(on_diagonal, 1.0 / jnp.where(on_diagonal, old, 1.0), 0.0)
            gradient = gradient - inverse
        trial = old - step_size * gradient
        shrunk = jnp.where(trial > edge, trial - edge, jnp.where(trial < -edge, trial + edge, 0.0))
        if kind == 0:
            shrunk = jnp.where(on_diagonal, trial, shrunk)
        out[0, strip[kind], s] = jnp.where(place >= 0, shrunk, 0.0)

    def finish_outer(kind):
        mirrors[kind].wait_recv()
        for s in range(share):
            finish(kind, s, mrecv[kind - 1, s].T)

    for kind in (2, 1):
        add_arrived(kind, 0, nr // 2)
        mirrors[kind].start()
    finish_outer(2)
    add_arrived(0, 0, nr // 2)
    for s in range(share):
        if paired_here:
            other = s + lax.div(r * share, TB) * (1 - 2 * (s % 2))
            finish(0, s, fbuf[0, 0, other].T)
        else:
            finish(0, s, None)
    finish_outer(1)
    for copy in row_copies.values():
        copy.wait_send()
    for copy in mirrors.values():
        copy.wait_send()


def solution(mesh):
    nr, nc = mesh.shape["row"], mesh.shape["col"]

    def on_device(observations, omega, block_slots):
        samples, width = observations.shape
        kmax = omega.shape[2]
        share = kmax // nr
        vmem, here = pl.BlockSpec(memory_space=pltpu.VMEM), pl.BlockSpec(memory_space=pltpu.HBM)
        dma = pltpu.SemaphoreType.DMA
        return pl.pallas_call(
            functools.partial(kernel, nr, nc, kmax),
            out_shape=jax.ShapeDtypeStruct((1, 3, share, BLK, BLK), f32),
            in_specs=[pl.BlockSpec(memory_space=pltpu.SMEM), here, here],
            out_specs=vmem,
            scratch_shapes=[
                pltpu.SMEM((3, kmax + TB), jnp.int32),
                pltpu.VMEM((samples, width), f32),
                pltpu.VMEM(omega.shape, f32),
                pltpu.VMEM((samples, width), f32),
                pltpu.VMEM((samples, width), f32),
                pltpu.VMEM((3 * TB, samples, 2 * BLK), bf16),
                pltpu.VMEM((3 * TB, 2 * BLK, samples), bf16),
                pltpu.VMEM((3 * kmax, 2 * BLK, 2 * BLK), bf16),
                pltpu.VMEM((3 * (kmax + 1), samples, BLK), f32),
                pltpu.VMEM((TB, samples, 2 * BLK), bf16),
                pltpu.VMEM((3, nr, share, BLK, BLK), f32),
                pltpu.VMEM((3, nr - 1, share, BLK, BLK), f32),
                pltpu.VMEM((2, share, BLK, BLK), f32),
                dma((2,)),
                dma((CHUNKS,)),
                dma((CHUNKS,)),
                dma((CHUNKS,)),
                dma((CHUNKS,)),
                dma((3, nr - 1)),
                dma((3, nr - 1)),
                dma((2,)),
                dma((2,)),
            ],
            compiler_params=pltpu.CompilerParams(
                collective_id=0, has_side_effects=True, vmem_limit_bytes=40 * 1024 * 1024
            ),
        )(jnp.transpose(block_slots, (1, 0, 2)), observations, omega)

    return jax.shard_map(
        on_device,
        mesh=mesh,
        in_specs=(P("row", "col"), P("col", None, None, None, None), P("col", None, None)),
        out_specs=P("col", None, "row", None, None),
        check_vma=False,
    )
```

```python
import functools

import jax
import jax.numpy as jnp
from jax import lax
from jax.experimental import pallas as pl
from jax.experimental.pallas import tpu as pltpu
from jax.sharding import PartitionSpec as P

MESH = pl.DeviceIdType.MESH
BLK = 128
TB = 8
CHUNKS = 16
WINDOW = 4

step_size = 0.5
penalty = 0.1
f32, bf16 = jnp.float32, jnp.bfloat16


def split(value):
    high = value.astype(bf16)
    return high, (value - high.astype(f32)).astype(bf16)


def flip(index, mask):
    out, bit = index, 1
    while bit <= mask:
        if mask & bit:
            out = out + bit * (1 - 2 * lax.rem(lax.div(index, bit), 2))
        bit *= 2
    return out


def kernel(
    nr, nc, kmax, slots, obs_in, omega_in, out, tab, obs, omega, near, far, xs, xt, wcat, cum, rs, fbuf, rbuf,
    mrecv, load, near_send, near_recv, far_send, far_recv, row_send, row_recv, mir_send, mir_recv,
):
    samples = obs_in.shape[0]
    load_obs = pltpu.make_async_copy(obs_in, obs, load.at[0])
    load_omega = pltpu.make_async_copy(omega_in, omega, load.at[1])
    share = kmax // nr
    bits = nr.bit_length() - 1
    r, c = lax.axis_index("row"), lax.axis_index("col")
    odd = lax.rem(c, 2)
    near_col = c + 1 - 2 * odd
    far_col = lax.rem(c - 1 + 2 * odd + nc, nc)
    relay_to = lax.rem(c + 2 - 4 * odd + nc, nc)
    relay_from = lax.rem(c - 2 + 4 * odd + nc, nc)
    strip = (1, 2 - 2 * odd, 2 * odd)

    barrier = pltpu.get_barrier_semaphore()
    partners = [{"col": near_col}, {"col": far_col}, {"col": relay_from}]
    partners += [{"row": flip(r, 1 << k)} for k in range(bits)]
    for partner in partners:
        pl.semaphore_signal(barrier, inc=1, device_id=partner, device_id_type=MESH)
    pl.semaphore_wait(barrier, len(partners))

    piece = samples // CHUNKS

    def near_copy(k):
        rows = pl.ds(k * piece, piece)
        return pltpu.make_async_remote_copy(
            obs_in.at[rows], near.at[rows], near_send.at[k], near_recv.at[k],
            device_id={"col": near_col}, device_id_type=MESH,
        )

    def far_copy(k):
        rows = pl.ds(k * piece, piece)
        return pltpu.make_async_remote_copy(
            near.at[rows], far.at[rows], far_send.at[k], far_recv.at[k],
            device_id={"col": relay_to}, device_id_type=MESH,
        )

    near_copies = [near_copy(k) for k in range(CHUNKS)]
    far_copies = [far_copy(k) for k in range(CHUNKS)]
    for copy in near_copies[:WINDOW]:
        copy.start()
    load_obs.start()
    load_omega.start()

    def relay(k):
        near_copies[k].wait_recv()
        far_copies[k].start()
        near_copies[k].wait_send()
        if k + WINDOW < CHUNKS:
            near_copies[k + WINDOW].start()

    def convert(source, kind, first, count):
        rows = pl.ds(first, count)
        for a in range(TB):
            block = source[rows, pl.ds(a * BLK, BLK)]
            high, low = split(block)
            xs[kind * TB + a, rows, :] = jnp.concatenate([high, low], axis=1)
            high, low = split(block.T)
            xt[kind * TB + a, :, rows] = jnp.concatenate([high, low], axis=0)

    def fill(e, _):
        places = [slots[e, 0, j] for j in range(kmax)]
        columns = [jnp.where(p >= 0, lax.rem(jnp.maximum(p, 0), TB), TB) for p in places]
        for j in range(kmax):
            before = jnp.int32(kmax)
            for i in range(j):
                before = jnp.where(columns[i] == columns[j], i, before)
            tab[e, j] = before
        for b in range(TB):
            last = jnp.int32(kmax)
            for j in range(kmax):
                last = jnp.where(columns[j] == b, j, last)
            tab[e, kmax + b] = last
        return 0

    def entry(kind, at):
        return tab[strip[kind], at]

    def position(kind, slot):
        return slots[strip[kind], 0, slot]

    def weights(kind):
        def body(slot, _):
            live = position(kind, slot) >= 0
            high, low = split(jnp.where(live, omega[0, strip[kind], slot], 0.0))
            top = jnp.concatenate([high, low], axis=1)
            bottom = jnp.concatenate([high, jnp.zeros_like(low)], axis=1)
            wcat[kind * kmax + slot] = jnp.concatenate([top, bottom], axis=0)
            return 0

        lax.fori_loop(0, kmax, body, 0, unroll=2)
        cum[kind * (kmax + 1) + kmax] = jnp.zeros((samples, BLK), f32)

    def products(kind, first, count):
        rows = pl.ds(first, count)

        def body(slot, _):
            a = lax.div(jnp.maximum(position(kind, slot), 0), TB)
            both = jnp.dot(
                xs[kind * TB + a, rows, :], wcat[kind * kmax + slot], preferred_element_type=f32
            )
            before = cum[kind * (kmax + 1) + entry(kind, slot), rows, :]
            cum[kind * (kmax + 1) + slot, rows, :] = before + (both[:, :BLK] + both[:, BLK:])
            return 0

        lax.fori_loop(0, kmax, body, 0, unroll=4)

    piece_rows = samples // CHUNKS
    half, quarter = samples // 2, samples // 4
    done = 0

    def relay_to_row(row):
        nonlocal done
        while done < row // piece_rows:
            relay(done)
            done += 1

    def relay_next():
        nonlocal done
        if done < CHUNKS:
            relay(done)
            done += 1

    lax.fori_loop(0, 3, fill, 0)
    load_obs.wait()
    convert(obs, 0, 0, half)
    relay_next()
    convert(obs, 0, half, half)
    relay_next()
    load_omega.wait()
    weights(0)
    relay_next()
    products(0, 0, half)
    relay_next()
    products(0, half, half)
    relay_next()
    weights(1)
    relay_next()
    weights(2)
    for first, count in ((0, half), (half, quarter), (half + quarter, quarter)):
        relay_to_row(first + count)
        convert(near, 1, first, count)
        relay_next()
        products(1, first, count)
        relay_next()
        for k in range(first // piece_rows, (first + count) // piece_rows):
            far_copies[k].wait_recv()
        convert(far, 2, first, count)
        relay_next()
        products(2, first, count)
    for copy in far_copies:
        copy.wait_send()

    def collect(b, _):
        total = cum[entry(0, kmax + b)]
        for kind in (1, 2):
            total = total + cum[kind * (kmax + 1) + entry(kind, kmax + b)]
        high, low = split(total)
        rs[b] = jnp.concatenate([high, low], axis=1)
        return 0

    lax.fori_loop(0, TB, collect, 0, unroll=2)

    def forward(kind, slot):
        place = jnp.maximum(position(kind, slot), 0)
        both = jnp.dot(
            xt[kind * TB + lax.div(place, TB)], rs[lax.rem(place, TB)], preferred_element_type=f32
        )
        both = both[:BLK] + both[BLK:]
        return both[:, :BLK] + both[:, BLK:]

    def mate(slot):
        return slot + lax.div(slot, TB) * (1 - 2 * lax.rem(slot, 2))

    paired_here = share % 2 == 0
    parts = 2 if paired_here else 1
    size = share // parts

    def row_copy(kind, q, p):
        bit = q & -q
        part = pl.ds(p * size, size)
        return pltpu.make_async_remote_copy(
            fbuf.at[kind, q, part], rbuf.at[kind, q - 1, part], row_send.at[kind, q - 1, p],
            row_recv.at[kind, q - 1, p], device_id={"row": flip(r, bit)}, device_id_type=MESH,
        )

    row_copies = {
        (kind, q, p): row_copy(kind, q, p) for kind in range(3) for q in range(1, nr) for p in range(parts)
    }

    def group(kind, q, p):
        first = flip(r, q) * share

        def body(s, _):
            value = forward(kind, first + s)
            if kind == 0 and not paired_here:
                value = value + forward(kind, mate(first + s)).T
            fbuf[kind, q, s] = value
            return 0

        lax.fori_loop(p * size, (p + 1) * size, body, 0, unroll=True)

    def add_arrived(kind, q, bit, p):
        row_copies[kind, q | bit, p].wait_recv()
        part = pl.ds(p * size, size)
        fbuf[kind, q, part] = fbuf[kind, q, part] + rbuf[kind, (q | bit) - 1, part]

    def reduce(kind, q, p):
        group(kind, q, p)
        low = q & -q if q else nr // 2
        bit = 1
        while bit < low:
            add_arrived(kind, q, bit, p)
            bit *= 2
        if q:
            row_copies[kind, q, p].start()

    order = (2, 1, 0)
    for kind in order:
        for p in range(parts):
            for q in range(nr - 1, nr // 2 - 1, -1):
                reduce(kind, q, p)
    for kind in order:
        for p in range(parts):
            for q in range(nr // 2 - 1, -1, -1):
                reduce(kind, q, p)

    mirrors = {
        (kind, p): pltpu.make_async_remote_copy(
            fbuf.at[kind, 0, pl.ds(p * size, size)], mrecv.at[kind - 1, pl.ds(p * size, size)],
            mir_send.at[kind - 1, p], mir_recv.at[kind - 1, p],
            device_id={"col": near_col if kind == 1 else far_col}, device_id_type=MESH,
        )
        for kind in (1, 2)
        for p in range(parts)
    }
    scale = 0.5 / (samples * nr)
    eye = lax.broadcasted_iota(jnp.int32, (BLK, BLK), 0) == lax.broadcasted_iota(jnp.int32, (BLK, BLK), 1)

    def finish(kind, s, mirrored):
        slot = r * share + s
        place = position(kind, slot)
        gradient = fbuf[kind, 0, s] * scale if mirrored is None else (fbuf[kind, 0, s] + mirrored) * scale
        old = omega[0, strip[kind], slot]
        edge = step_size * penalty
        if kind == 0:
            on_diagonal = eye & (lax.div(place, TB) == lax.rem(place, TB)) & (place >= 0)
            inverse = jnp.where(on_diagonal, 1.0 / jnp.where(on_diagonal, old, 1.0), 0.0)
            gradient = gradient - inverse
        trial = old - step_size * gradient
        shrunk = jnp.where(trial > edge, trial - edge, jnp.where(trial < -edge, trial + edge, 0.0))
        if kind == 0:
            shrunk = jnp.where(on_diagonal, trial, shrunk)
        out[0, strip[kind], s] = jnp.where(place >= 0, shrunk, 0.0)

    def finish_outer(kind):
        for p in range(parts):
            mirrors[kind, p].wait_recv()
            for s in range(p * size, (p + 1) * size):
                finish(kind, s, mrecv[kind - 1, s].T)

    for kind in (2, 1):
        for p in range(parts):
            add_arrived(kind, 0, nr // 2, p)
            mirrors[kind, p].start()
    finish_outer(2)
    for p in range(parts):
        add_arrived(0, 0, nr // 2, p)
    for s in range(share):
        if paired_here:
            other = s + lax.div(r * share, TB) * (1 - 2 * (s % 2))
            finish(0, s, fbuf[0, 0, other].T)
        else:
            finish(0, s, None)
    finish_outer(1)
    for copy in row_copies.values():
        copy.wait_send()
    for copy in mirrors.values():
        copy.wait_send()


def solution(mesh):
    nr, nc = mesh.shape["row"], mesh.shape["col"]

    def on_device(observations, omega, block_slots):
        samples, width = observations.shape
        kmax = omega.shape[2]
        share = kmax // nr
        parts = 2 if share % 2 == 0 else 1
        vmem, here = pl.BlockSpec(memory_space=pltpu.VMEM), pl.BlockSpec(memory_space=pl.ANY)
        dma = pltpu.SemaphoreType.DMA
        return pl.pallas_call(
            functools.partial(kernel, nr, nc, kmax),
            out_shape=jax.ShapeDtypeStruct((1, 3, share, BLK, BLK), f32),
            in_specs=[pl.BlockSpec(memory_space=pltpu.SMEM), here, here],
            out_specs=vmem,
            scratch_shapes=[
                pltpu.SMEM((3, kmax + TB), jnp.int32),
                pltpu.VMEM((samples, width), f32),
                pltpu.VMEM(omega.shape, f32),
                pltpu.VMEM((samples, width), f32),
                pltpu.VMEM((samples, width), f32),
                pltpu.VMEM((3 * TB, samples, 2 * BLK), bf16),
                pltpu.VMEM((3 * TB, 2 * BLK, samples), bf16),
                pltpu.VMEM((3 * kmax, 2 * BLK, 2 * BLK), bf16),
                pltpu.VMEM((3 * (kmax + 1), samples, BLK), f32),
                pltpu.VMEM((TB, samples, 2 * BLK), bf16),
                pltpu.VMEM((3, nr, share, BLK, BLK), f32),
                pltpu.VMEM((3, nr - 1, share, BLK, BLK), f32),
                pltpu.VMEM((2, share, BLK, BLK), f32),
                dma((2,)),
                dma((CHUNKS,)),
                dma((CHUNKS,)),
                dma((CHUNKS,)),
                dma((CHUNKS,)),
                dma((3, nr - 1, parts)),
                dma((3, nr - 1, parts)),
                dma((2, parts)),
                dma((2, parts)),
            ],
            compiler_params=pltpu.CompilerParams(
                collective_id=0, has_side_effects=True, vmem_limit_bytes=56 * 1024 * 1024
            ),
        )(jnp.transpose(block_slots, (1, 0, 2)), observations, omega)

    return jax.shard_map(
        on_device,
        mesh=mesh,
        in_specs=(P("row", "col"), P("col", None, None, None, None), P("col", None, None)),
        out_specs=P("col", None, "row", None, None),
        check_vma=False,
    )
```

```python
import functools

import jax
import jax.numpy as jnp
from jax import lax
from jax.experimental import pallas as pl
from jax.experimental.pallas import tpu as pltpu
from jax.sharding import PartitionSpec as P

MESH = pl.DeviceIdType.MESH
BLK = 128
TB = 8
CHUNKS = 16
WINDOW = 4

step_size = 0.5
penalty = 0.1
f32, bf16 = jnp.float32, jnp.bfloat16


def split(value):
    high = value.astype(bf16)
    return high, (value - high.astype(f32)).astype(bf16)


def flip(index, mask):
    out, bit = index, 1
    while bit <= mask:
        if mask & bit:
            out = out + bit * (1 - 2 * lax.rem(lax.div(index, bit), 2))
        bit *= 2
    return out


def kernel(
    nr, nc, kmax, slots, obs_in, omega_in, out, tab, obs, omega, near, far, xs, xt, wcat, cum, rs, fbuf, rbuf,
    mrecv, load, near_send, near_recv, far_send, far_recv, row_send, row_recv, mir_send, mir_recv,
):
    samples = obs_in.shape[0]
    load_obs = pltpu.make_async_copy(obs_in, obs, load.at[0])
    load_omega = pltpu.make_async_copy(omega_in, omega, load.at[1])
    share = kmax // nr
    bits = nr.bit_length() - 1
    r, c = lax.axis_index("row"), lax.axis_index("col")
    odd = lax.rem(c, 2)
    near_col = c + 1 - 2 * odd
    far_col = lax.rem(c - 1 + 2 * odd + nc, nc)
    relay_to = lax.rem(c + 2 - 4 * odd + nc, nc)
    relay_from = lax.rem(c - 2 + 4 * odd + nc, nc)
    strip = (1, 2 - 2 * odd, 2 * odd)

    barrier = pltpu.get_barrier_semaphore()
    partners = [{"col": near_col}, {"col": far_col}, {"col": relay_from}]
    partners += [{"row": flip(r, 1 << k)} for k in range(bits)]
    for partner in partners:
        pl.semaphore_signal(barrier, inc=1, device_id=partner, device_id_type=MESH)
    pl.semaphore_wait(barrier, len(partners))

    piece = samples // CHUNKS

    def near_copy(k):
        rows = pl.ds(k * piece, piece)
        return pltpu.make_async_remote_copy(
            obs_in.at[rows], near.at[rows], near_send.at[k], near_recv.at[k],
            device_id={"col": near_col}, device_id_type=MESH,
        )

    def far_copy(k):
        rows = pl.ds(k * piece, piece)
        return pltpu.make_async_remote_copy(
            near.at[rows], far.at[rows], far_send.at[k], far_recv.at[k],
            device_id={"col": relay_to}, device_id_type=MESH,
        )

    near_copies = [near_copy(k) for k in range(CHUNKS)]
    far_copies = [far_copy(k) for k in range(CHUNKS)]
    for copy in near_copies[:WINDOW]:
        copy.start()
    load_obs.start()
    load_omega.start()

    def relay(k):
        near_copies[k].wait_recv()
        far_copies[k].start()
        near_copies[k].wait_send()
        if k + WINDOW < CHUNKS:
            near_copies[k + WINDOW].start()

    def convert(source, kind, first, count):
        rows = pl.ds(first, count)
        for a in range(TB):
            block = source[rows, pl.ds(a * BLK, BLK)]
            high, low = split(block)
            xs[kind * TB + a, rows, :] = jnp.concatenate([high, low], axis=1)
            high, low = split(block.T)
            xt[kind * TB + a, :, rows] = jnp.concatenate([high, low], axis=0)

    def fill(e, _):
        places = [slots[e, 0, j] for j in range(kmax)]
        columns = [jnp.where(p >= 0, lax.rem(jnp.maximum(p, 0), TB), TB) for p in places]
        for j in range(kmax):
            before = jnp.int32(kmax)
            for i in range(j):
                before = jnp.where(columns[i] == columns[j], i, before)
            tab[e, j] = before
        for b in range(TB):
            last = jnp.int32(kmax)
            for j in range(kmax):
                last = jnp.where(columns[j] == b, j, last)
            tab[e, kmax + b] = last
        return 0

    def entry(kind, at):
        return tab[strip[kind], at]

    def position(kind, slot):
        return slots[strip[kind], 0, slot]

    def weights(kind):
        def body(slot, _):
            live = position(kind, slot) >= 0
            high, low = split(jnp.where(live, omega[0, strip[kind], slot], 0.0))
            top = jnp.concatenate([high, low], axis=1)
            bottom = jnp.concatenate([high, jnp.zeros_like(low)], axis=1)
            wcat[kind * kmax + slot] = jnp.concatenate([top, bottom], axis=0)
            return 0

        lax.fori_loop(0, kmax, body, 0, unroll=4)
        cum[kind * (kmax + 1) + kmax] = jnp.zeros((samples, BLK), f32)

    def products(kind, first, count):
        rows = pl.ds(first, count)

        def body(slot, _):
            a = lax.div(jnp.maximum(position(kind, slot), 0), TB)
            both = jnp.dot(
                xs[kind * TB + a, rows, :], wcat[kind * kmax + slot], preferred_element_type=f32
            )
            before = cum[kind * (kmax + 1) + entry(kind, slot), rows, :]
            cum[kind * (kmax + 1) + slot, rows, :] = before + (both[:, :BLK] + both[:, BLK:])
            return 0

        lax.fori_loop(0, kmax, body, 0, unroll=8)

    piece_rows = samples // CHUNKS
    half = samples // 2
    done = 0

    def relay_to_row(row):
        nonlocal done
        while done < row // piece_rows:
            relay(done)
            done += 1

    def relay_next():
        nonlocal done
        if done < CHUNKS:
            relay(done)
            done += 1

    lax.fori_loop(0, 3, fill, 0)
    load_obs.wait()
    convert(obs, 0, 0, half)
    relay_next()
    convert(obs, 0, half, half)
    relay_next()
    load_omega.wait()
    weights(0)
    relay_next()
    products(0, 0, samples)
    relay_next()
    relay_next()
    weights(1)
    relay_next()
    weights(2)
    for first, count in ((0, half), (half, half)):
        relay_to_row(first + count)
        convert(near, 1, first, count)
        relay_next()
        products(1, first, count)
        relay_next()
        for k in range(first // piece_rows, (first + count) // piece_rows):
            far_copies[k].wait_recv()
        convert(far, 2, first, count)
        relay_next()
        products(2, first, count)
    for copy in far_copies:
        copy.wait_send()

    def collect(b, _):
        total = cum[entry(0, kmax + b)]
        for kind in (1, 2):
            total = total + cum[kind * (kmax + 1) + entry(kind, kmax + b)]
        high, low = split(total)
        rs[b] = jnp.concatenate([high, low], axis=1)
        return 0

    lax.fori_loop(0, TB, collect, 0, unroll=4)

    def forward(kind, slot):
        place = jnp.maximum(position(kind, slot), 0)
        both = jnp.dot(
            xt[kind * TB + lax.div(place, TB)], rs[lax.rem(place, TB)], preferred_element_type=f32
        )
        both = both[:BLK] + both[BLK:]
        return both[:, :BLK] + both[:, BLK:]

    def mate(slot):
        return slot + lax.div(slot, TB) * (1 - 2 * lax.rem(slot, 2))

    paired_here = share % 2 == 0

    def row_copy(kind, q):
        bit = q & -q
        return pltpu.make_async_remote_copy(
            fbuf.at[kind, q], rbuf.at[kind, q - 1], row_send.at[kind, q - 1],
            row_recv.at[kind, q - 1], device_id={"row": flip(r, bit)}, device_id_type=MESH,
        )

    row_copies = {(kind, q): row_copy(kind, q) for kind in range(3) for q in range(1, nr)}

    def group(kind, q):
        first = flip(r, q) * share

        def body(s, _):
            part = forward(kind, first + s)
            if kind == 0 and not paired_here:
                part = part + forward(kind, mate(first + s)).T
            fbuf[kind, q, s] = part
            return 0

        lax.fori_loop(0, share, body, 0, unroll=True)

    def add_arrived(kind, q, bit):
        row_copies[kind, q | bit].wait_recv()
        fbuf[kind, q] = fbuf[kind, q] + rbuf[kind, (q | bit) - 1]

    def reduce(kind, q):
        group(kind, q)
        low = q & -q if q else nr // 2
        bit = 1
        while bit < low:
            add_arrived(kind, q, bit)
            bit *= 2
        if q:
            row_copies[kind, q].start()

    order = (2, 1, 0)
    for kind in order:
        for q in range(nr - 1, nr // 2 - 1, -1):
            reduce(kind, q)
    for kind in order:
        for q in range(nr // 2 - 1, -1, -1):
            reduce(kind, q)

    mirrors = {
        kind: pltpu.make_async_remote_copy(
            fbuf.at[kind, 0], mrecv.at[kind - 1], mir_send.at[kind - 1], mir_recv.at[kind - 1],
            device_id={"col": near_col if kind == 1 else far_col}, device_id_type=MESH,
        )
        for kind in (1, 2)
    }
    scale = 0.5 / (samples * nr)
    eye = lax.broadcasted_iota(jnp.int32, (BLK, BLK), 0) == lax.broadcasted_iota(jnp.int32, (BLK, BLK), 1)

    def finish(kind, s, mirrored):
        slot = r * share + s
        place = position(kind, slot)
        gradient = fbuf[kind, 0, s] * scale if mirrored is None else (fbuf[kind, 0, s] + mirrored) * scale
        old = omega[0, strip[kind], slot]
        edge = step_size * penalty
        if kind == 0:
            on_diagonal = eye & (lax.div(place, TB) == lax.rem(place, TB)) & (place >= 0)
            inverse = jnp.where(on_diagonal, 1.0 / jnp.where(on_diagonal, old, 1.0), 0.0)
            gradient = gradient - inverse
        trial = old - step_size * gradient
        shrunk = jnp.where(trial > edge, trial - edge, jnp.where(trial < -edge, trial + edge, 0.0))
        if kind == 0:
            shrunk = jnp.where(on_diagonal, trial, shrunk)
        out[0, strip[kind], s] = jnp.where(place >= 0, shrunk, 0.0)

    def finish_outer(kind):
        mirrors[kind].wait_recv()
        for s in range(share):
            finish(kind, s, mrecv[kind - 1, s].T)

    for kind in (2, 1):
        add_arrived(kind, 0, nr // 2)
        mirrors[kind].start()
    finish_outer(2)
    add_arrived(0, 0, nr // 2)
    for s in range(share):
        if paired_here:
            other = s + lax.div(r * share, TB) * (1 - 2 * (s % 2))
            finish(0, s, fbuf[0, 0, other].T)
        else:
            finish(0, s, None)
    finish_outer(1)
    for copy in row_copies.values():
        copy.wait_send()
    for copy in mirrors.values():
        copy.wait_send()


def solution(mesh):
    nr, nc = mesh.shape["row"], mesh.shape["col"]

    def on_device(observations, omega, block_slots):
        samples, width = observations.shape
        kmax = omega.shape[2]
        share = kmax // nr
        vmem, here = pl.BlockSpec(memory_space=pltpu.VMEM), pl.BlockSpec(memory_space=pl.ANY)
        dma = pltpu.SemaphoreType.DMA
        return pl.pallas_call(
            functools.partial(kernel, nr, nc, kmax),
            out_shape=jax.ShapeDtypeStruct((1, 3, share, BLK, BLK), f32),
            in_specs=[pl.BlockSpec(memory_space=pltpu.SMEM), here, here],
            out_specs=vmem,
            scratch_shapes=[
                pltpu.SMEM((3, kmax + TB), jnp.int32),
                pltpu.VMEM((samples, width), f32),
                pltpu.VMEM(omega.shape, f32),
                pltpu.VMEM((samples, width), f32),
                pltpu.VMEM((samples, width), f32),
                pltpu.VMEM((3 * TB, samples, 2 * BLK), bf16),
                pltpu.VMEM((3 * TB, 2 * BLK, samples), bf16),
                pltpu.VMEM((3 * kmax, 2 * BLK, 2 * BLK), bf16),
                pltpu.VMEM((3 * (kmax + 1), samples, BLK), f32),
                pltpu.VMEM((TB, samples, 2 * BLK), bf16),
                pltpu.VMEM((3, nr, share, BLK, BLK), f32),
                pltpu.VMEM((3, nr - 1, share, BLK, BLK), f32),
                pltpu.VMEM((2, share, BLK, BLK), f32),
                dma((2,)),
                dma((CHUNKS,)),
                dma((CHUNKS,)),
                dma((CHUNKS,)),
                dma((CHUNKS,)),
                dma((3, nr - 1)),
                dma((3, nr - 1)),
                dma((2,)),
                dma((2,)),
            ],
            compiler_params=pltpu.CompilerParams(
                collective_id=0, has_side_effects=True, vmem_limit_bytes=56 * 1024 * 1024
            ),
        )(jnp.transpose(block_slots, (1, 0, 2)), observations, omega)

    return jax.shard_map(
        on_device,
        mesh=mesh,
        in_specs=(P("row", "col"), P("col", None, None, None, None), P("col", None, None)),
        out_specs=P("col", None, "row", None, None),
        check_vma=False,
    )
```

```python
import functools

import jax
import jax.numpy as jnp
from jax import lax
from jax.experimental import pallas as pl
from jax.experimental.pallas import tpu as pltpu
from jax.sharding import PartitionSpec as P

MESH = pl.DeviceIdType.MESH
BLK = 128
TB = 8
CHUNKS = 16
STEP = 4
WINDOW = 4

step_size = 0.5
penalty = 0.1
f32, bf16 = jnp.float32, jnp.bfloat16


def split(value):
    high = value.astype(bf16)
    return high, (value - high.astype(f32)).astype(bf16)


def flip(index, mask):
    out, bit = index, 1
    while bit <= mask:
        if mask & bit:
            out = out + bit * (1 - 2 * lax.rem(lax.div(index, bit), 2))
        bit *= 2
    return out


def kernel(
    nr, nc, kmax, slots, obs_in, omega_in, out, tab, obs, omega, near, far, xs, xt, wcat, cum, rs, fbuf, rbuf,
    mrecv, load, near_send, near_recv, far_send, far_recv, row_send, row_recv, mir_send, mir_recv,
):
    samples = obs_in.shape[0]
    load_obs = pltpu.make_async_copy(obs_in, obs, load.at[0])
    load_omega = pltpu.make_async_copy(omega_in, omega, load.at[1])
    share = kmax // nr
    bits = nr.bit_length() - 1
    r, c = lax.axis_index("row"), lax.axis_index("col")
    odd = lax.rem(c, 2)
    near_col = c + 1 - 2 * odd
    far_col = lax.rem(c - 1 + 2 * odd + nc, nc)
    relay_to = lax.rem(c + 2 - 4 * odd + nc, nc)
    relay_from = lax.rem(c - 2 + 4 * odd + nc, nc)
    strip = (1, 2 - 2 * odd, 2 * odd)

    barrier = pltpu.get_barrier_semaphore()
    partners = [{"col": near_col}, {"col": far_col}, {"col": relay_from}]
    partners += [{"row": flip(r, 1 << k)} for k in range(bits)]
    for partner in partners:
        pl.semaphore_signal(barrier, inc=1, device_id=partner, device_id_type=MESH)
    pl.semaphore_wait(barrier, len(partners))

    piece = samples // CHUNKS

    def near_copy(k):
        rows = pl.ds(k * piece, piece)
        return pltpu.make_async_remote_copy(
            obs_in.at[rows], near.at[rows], near_send.at[k], near_recv.at[k],
            device_id={"col": near_col}, device_id_type=MESH,
        )

    def far_copy(k):
        rows = pl.ds(k * piece, piece)
        return pltpu.make_async_remote_copy(
            near.at[rows], far.at[rows], far_send.at[k], far_recv.at[k],
            device_id={"col": relay_to}, device_id_type=MESH,
        )

    near_copies = [near_copy(k) for k in range(CHUNKS)]
    far_copies = [far_copy(k) for k in range(CHUNKS)]
    for copy in near_copies[:WINDOW]:
        copy.start()
    load_obs.start()
    load_omega.start()

    def relay(k):
        near_copies[k].wait_recv()
        far_copies[k].start()
        near_copies[k].wait_send()
        if k + WINDOW < CHUNKS:
            near_copies[k + WINDOW].start()

    def convert(source, kind, first, count):
        rows = pl.ds(first, count)
        for a in range(TB):
            block = source[rows, pl.ds(a * BLK, BLK)]
            high, low = split(block)
            xs[kind * TB + a, rows, :] = jnp.concatenate([high, low], axis=1)
            high, low = split(block.T)
            xt[kind * TB + a, :, rows] = jnp.concatenate([high, low], axis=0)

    def fill(e, _):
        places = [slots[e, 0, j] for j in range(kmax)]
        columns = [jnp.where(p >= 0, lax.rem(jnp.maximum(p, 0), TB), TB) for p in places]
        for j in range(kmax):
            before = jnp.int32(kmax)
            for i in range(j):
                before = jnp.where(columns[i] == columns[j], i, before)
            tab[e, j] = before
        for b in range(TB):
            last = jnp.int32(kmax)
            for j in range(kmax):
                last = jnp.where(columns[j] == b, j, last)
            tab[e, kmax + b] = last
        return 0

    def entry(kind, at):
        return tab[strip[kind], at]

    def position(kind, slot):
        return slots[strip[kind], 0, slot]

    def weights(kind):
        def body(step, _):
            built = []
            for i in range(STEP):
                slot = step * STEP + i
                live = position(kind, slot) >= 0
                built.append(split(jnp.where(live, omega[0, strip[kind], slot], 0.0)))
            for i, (high, low) in enumerate(built):
                top = jnp.concatenate([high, low], axis=1)
                bottom = jnp.concatenate([high, jnp.zeros_like(low)], axis=1)
                wcat[kind * kmax + step * STEP + i] = jnp.concatenate([top, bottom], axis=0)
            return 0

        lax.fori_loop(0, kmax // STEP, body, 0)
        cum[kind * (kmax + 1) + kmax] = jnp.zeros((samples, BLK), f32)

    def products(kind, first, count):
        rows = pl.ds(first, count)

        def body(step, _):
            made = []
            for i in range(STEP):
                slot = step * STEP + i
                a = lax.div(jnp.maximum(position(kind, slot), 0), TB)
                both = jnp.dot(
                    xs[kind * TB + a, rows, :], wcat[kind * kmax + slot], preferred_element_type=f32
                )
                made.append(both[:, :BLK] + both[:, BLK:])
            for i, value in enumerate(made):
                slot = step * STEP + i
                before = cum[kind * (kmax + 1) + entry(kind, slot), rows, :]
                cum[kind * (kmax + 1) + slot, rows, :] = before + value
            return 0

        lax.fori_loop(0, kmax // STEP, body, 0, unroll=2)

    piece_rows = samples // CHUNKS
    half = samples // 2
    done = 0

    def relay_to_row(row):
        nonlocal done
        while done < row // piece_rows:
            relay(done)
            done += 1

    def relay_next():
        nonlocal done
        if done < CHUNKS:
            relay(done)
            done += 1

    lax.fori_loop(0, 3, fill, 0)
    load_obs.wait()
    convert(obs, 0, 0, half)
    relay_next()
    convert(obs, 0, half, half)
    relay_next()
    load_omega.wait()
    weights(0)
    relay_next()
    products(0, 0, half)
    products(0, half, half)
    relay_next()
    relay_next()
    weights(1)
    relay_next()
    weights(2)
    for first, count in ((0, half), (half, half)):
        relay_to_row(first + count)
        convert(near, 1, first, count)
        relay_next()
        products(1, first, count)
        relay_next()
        for k in range(first // piece_rows, (first + count) // piece_rows):
            far_copies[k].wait_recv()
        convert(far, 2, first, count)
        relay_next()
        products(2, first, count)
    for copy in far_copies:
        copy.wait_send()

    for first in (0, half):
        rows = pl.ds(first, half)
        for start in range(0, TB, STEP):
            sums = []
            for b in range(start, start + STEP):
                total = cum[entry(0, kmax + b), rows, :]
                for kind in (1, 2):
                    total = total + cum[kind * (kmax + 1) + entry(kind, kmax + b), rows, :]
                sums.append(total)
            for i, total in enumerate(sums):
                high, low = split(total)
                rs[start + i, rows, :] = jnp.concatenate([high, low], axis=1)

    def forward(kind, slot):
        place = jnp.maximum(position(kind, slot), 0)
        both = jnp.dot(
            xt[kind * TB + lax.div(place, TB)], rs[lax.rem(place, TB)], preferred_element_type=f32
        )
        both = both[:BLK] + both[BLK:]
        return both[:, :BLK] + both[:, BLK:]

    def mate(slot):
        return slot + lax.div(slot, TB) * (1 - 2 * lax.rem(slot, 2))

    paired_here = share % 2 == 0

    def row_copy(kind, q):
        bit = q & -q
        return pltpu.make_async_remote_copy(
            fbuf.at[kind, q], rbuf.at[kind, q - 1], row_send.at[kind, q - 1],
            row_recv.at[kind, q - 1], device_id={"row": flip(r, bit)}, device_id_type=MESH,
        )

    row_copies = {(kind, q): row_copy(kind, q) for kind in range(3) for q in range(1, nr)}

    def group(kind, q):
        first = flip(r, q) * share

        values = []
        for s in range(share):
            part = forward(kind, first + s)
            if kind == 0 and not paired_here:
                part = part + forward(kind, mate(first + s)).T
            values.append(part)
        for s, part in enumerate(values):
            fbuf[kind, q, s] = part

    def add_arrived(kind, q, bit):
        row_copies[kind, q | bit].wait_recv()
        fbuf[kind, q] = fbuf[kind, q] + rbuf[kind, (q | bit) - 1]

    def reduce(kind, q):
        group(kind, q)
        low = q & -q if q else nr // 2
        bit = 1
        while bit < low:
            add_arrived(kind, q, bit)
            bit *= 2
        if q:
            row_copies[kind, q].start()

    order = (2, 1, 0)
    for kind in order:
        for q in range(nr - 1, nr // 2 - 1, -1):
            reduce(kind, q)
    for kind in order:
        for q in range(nr // 2 - 1, -1, -1):
            reduce(kind, q)

    mirrors = {
        kind: pltpu.make_async_remote_copy(
            fbuf.at[kind, 0], mrecv.at[kind - 1], mir_send.at[kind - 1], mir_recv.at[kind - 1],
            device_id={"col": near_col if kind == 1 else far_col}, device_id_type=MESH,
        )
        for kind in (1, 2)
    }
    scale = 0.5 / (samples * nr)
    eye = lax.broadcasted_iota(jnp.int32, (BLK, BLK), 0) == lax.broadcasted_iota(jnp.int32, (BLK, BLK), 1)

    def finish(kind, s, mirrored):
        slot = r * share + s
        place = position(kind, slot)
        gradient = fbuf[kind, 0, s] * scale if mirrored is None else (fbuf[kind, 0, s] + mirrored) * scale
        old = omega[0, strip[kind], slot]
        edge = step_size * penalty
        if kind == 0:
            on_diagonal = eye & (lax.div(place, TB) == lax.rem(place, TB)) & (place >= 0)
            inverse = jnp.where(on_diagonal, 1.0 / jnp.where(on_diagonal, old, 1.0), 0.0)
            gradient = gradient - inverse
        trial = old - step_size * gradient
        shrunk = jnp.where(trial > edge, trial - edge, jnp.where(trial < -edge, trial + edge, 0.0))
        if kind == 0:
            shrunk = jnp.where(on_diagonal, trial, shrunk)
        out[0, strip[kind], s] = jnp.where(place >= 0, shrunk, 0.0)

    def finish_outer(kind):
        mirrors[kind].wait_recv()
        for s in range(share):
            finish(kind, s, mrecv[kind - 1, s].T)

    for kind in (2, 1):
        add_arrived(kind, 0, nr // 2)
        mirrors[kind].start()
    finish_outer(2)
    add_arrived(0, 0, nr // 2)
    for s in range(share):
        if paired_here:
            other = s + lax.div(r * share, TB) * (1 - 2 * (s % 2))
            finish(0, s, fbuf[0, 0, other].T)
        else:
            finish(0, s, None)
    finish_outer(1)
    for copy in row_copies.values():
        copy.wait_send()
    for copy in mirrors.values():
        copy.wait_send()


def solution(mesh):
    nr, nc = mesh.shape["row"], mesh.shape["col"]

    def on_device(observations, omega, block_slots):
        samples, width = observations.shape
        kmax = omega.shape[2]
        share = kmax // nr
        vmem, here = pl.BlockSpec(memory_space=pltpu.VMEM), pl.BlockSpec(memory_space=pl.ANY)
        dma = pltpu.SemaphoreType.DMA
        return pl.pallas_call(
            functools.partial(kernel, nr, nc, kmax),
            out_shape=jax.ShapeDtypeStruct((1, 3, share, BLK, BLK), f32),
            in_specs=[pl.BlockSpec(memory_space=pltpu.SMEM), here, here],
            out_specs=vmem,
            scratch_shapes=[
                pltpu.SMEM((3, kmax + TB), jnp.int32),
                pltpu.VMEM((samples, width), f32),
                pltpu.VMEM(omega.shape, f32),
                pltpu.VMEM((samples, width), f32),
                pltpu.VMEM((samples, width), f32),
                pltpu.VMEM((3 * TB, samples, 2 * BLK), bf16),
                pltpu.VMEM((3 * TB, 2 * BLK, samples), bf16),
                pltpu.VMEM((3 * kmax, 2 * BLK, 2 * BLK), bf16),
                pltpu.VMEM((3 * (kmax + 1), samples, BLK), f32),
                pltpu.VMEM((TB, samples, 2 * BLK), bf16),
                pltpu.VMEM((3, nr, share, BLK, BLK), f32),
                pltpu.VMEM((3, nr - 1, share, BLK, BLK), f32),
                pltpu.VMEM((2, share, BLK, BLK), f32),
                dma((2,)),
                dma((CHUNKS,)),
                dma((CHUNKS,)),
                dma((CHUNKS,)),
                dma((CHUNKS,)),
                dma((3, nr - 1)),
                dma((3, nr - 1)),
                dma((2,)),
                dma((2,)),
            ],
            compiler_params=pltpu.CompilerParams(
                collective_id=0, has_side_effects=True, vmem_limit_bytes=56 * 1024 * 1024
            ),
        )(jnp.transpose(block_slots, (1, 0, 2)), observations, omega)

    return jax.shard_map(
        on_device,
        mesh=mesh,
        in_specs=(P("row", "col"), P("col", None, None, None, None), P("col", None, None)),
        out_specs=P("col", None, "row", None, None),
        check_vma=False,
    )
```

```python
import functools

import jax
import jax.numpy as jnp
from jax import lax
from jax.experimental import pallas as pl
from jax.experimental.pallas import tpu as pltpu
from jax.sharding import PartitionSpec as P

MESH = pl.DeviceIdType.MESH
BLK = 128
TB = 8
CHUNKS = 16
STEP = 4
WINDOW = 4

step_size = 0.5
penalty = 0.1
f32, bf16 = jnp.float32, jnp.bfloat16


def split(value):
    high = value.astype(bf16)
    return high, (value - high.astype(f32)).astype(bf16)


def flip(index, mask):
    out, bit = index, 1
    while bit <= mask:
        if mask & bit:
            out = out + bit * (1 - 2 * lax.rem(lax.div(index, bit), 2))
        bit *= 2
    return out


def kernel(
    nr, nc, kmax, slots, obs_in, omega_in, out, tab, obs, omega, near, far, xs, xt, wcat, cum, rs, fbuf, rbuf,
    mrecv, load, near_send, near_recv, far_send, far_recv, row_send, row_recv, mir_send, mir_recv,
):
    samples = obs_in.shape[0]
    load_obs = pltpu.make_async_copy(obs_in, obs, load.at[0])
    load_omega = pltpu.make_async_copy(omega_in, omega, load.at[1])
    share = kmax // nr
    bits = nr.bit_length() - 1
    r, c = lax.axis_index("row"), lax.axis_index("col")
    odd = lax.rem(c, 2)
    near_col = c + 1 - 2 * odd
    far_col = lax.rem(c - 1 + 2 * odd + nc, nc)
    relay_to = lax.rem(c + 2 - 4 * odd + nc, nc)
    relay_from = lax.rem(c - 2 + 4 * odd + nc, nc)
    strip = (1, 2 - 2 * odd, 2 * odd)

    barrier = pltpu.get_barrier_semaphore()
    partners = [{"col": near_col}, {"col": far_col}, {"col": relay_from}]
    partners += [{"row": flip(r, 1 << k)} for k in range(bits)]
    for partner in partners:
        pl.semaphore_signal(barrier, inc=1, device_id=partner, device_id_type=MESH)
    load_obs.start()
    load_omega.start()
    pl.semaphore_wait(barrier, len(partners))

    piece = samples // CHUNKS

    def near_copy(k):
        rows = pl.ds(k * piece, piece)
        return pltpu.make_async_remote_copy(
            obs_in.at[rows], near.at[rows], near_send.at[k], near_recv.at[k],
            device_id={"col": near_col}, device_id_type=MESH,
        )

    def far_copy(k):
        rows = pl.ds(k * piece, piece)
        return pltpu.make_async_remote_copy(
            near.at[rows], far.at[rows], far_send.at[k], far_recv.at[k],
            device_id={"col": relay_to}, device_id_type=MESH,
        )

    near_copies = [near_copy(k) for k in range(CHUNKS)]
    far_copies = [far_copy(k) for k in range(CHUNKS)]
    for copy in near_copies[:WINDOW]:
        copy.start()

    def relay(k):
        near_copies[k].wait_recv()
        far_copies[k].start()
        near_copies[k].wait_send()
        if k + WINDOW < CHUNKS:
            near_copies[k + WINDOW].start()

    def convert(source, kind, first, count):
        rows = pl.ds(first, count)
        for a in range(TB):
            block = source[rows, pl.ds(a * BLK, BLK)]
            high, low = split(block)
            xs[kind * TB + a, rows, :] = jnp.concatenate([high, low], axis=1)
            high, low = split(block.T)
            xt[kind * TB + a, :, rows] = jnp.concatenate([high, low], axis=0)

    def fill(e, _):
        places = [slots[e, 0, j] for j in range(kmax)]
        columns = [jnp.where(p >= 0, lax.rem(jnp.maximum(p, 0), TB), TB) for p in places]
        for j in range(kmax):
            before = jnp.int32(kmax)
            for i in range(j):
                before = jnp.where(columns[i] == columns[j], i, before)
            tab[e, j] = before
        for b in range(TB):
            last = jnp.int32(kmax)
            for j in range(kmax):
                last = jnp.where(columns[j] == b, j, last)
            tab[e, kmax + b] = last
        return 0

    def entry(kind, at):
        return tab[strip[kind], at]

    def position(kind, slot):
        return slots[strip[kind], 0, slot]

    def weights(kind):
        def body(step, _):
            built = []
            for i in range(STEP):
                slot = step * STEP + i
                live = position(kind, slot) >= 0
                built.append(split(jnp.where(live, omega[0, strip[kind], slot], 0.0)))
            for i, (high, low) in enumerate(built):
                top = jnp.concatenate([high, low], axis=1)
                bottom = jnp.concatenate([high, jnp.zeros_like(low)], axis=1)
                wcat[kind * kmax + step * STEP + i] = jnp.concatenate([top, bottom], axis=0)
            return 0

        lax.fori_loop(0, kmax // STEP, body, 0)
        cum[kind * (kmax + 1) + kmax] = jnp.zeros((samples, BLK), f32)

    def products(kind, first, count):
        rows = pl.ds(first, count)

        def body(step, _):
            made = []
            for i in range(STEP):
                slot = step * STEP + i
                a = lax.div(jnp.maximum(position(kind, slot), 0), TB)
                both = jnp.dot(
                    xs[kind * TB + a, rows, :], wcat[kind * kmax + slot], preferred_element_type=f32
                )
                made.append(both[:, :BLK] + both[:, BLK:])
            for i, value in enumerate(made):
                slot = step * STEP + i
                before = cum[kind * (kmax + 1) + entry(kind, slot), rows, :]
                cum[kind * (kmax + 1) + slot, rows, :] = before + value
            return 0

        lax.fori_loop(0, kmax // STEP, body, 0, unroll=2)

    piece_rows = samples // CHUNKS
    half = samples // 2
    done = 0

    def relay_to_row(row):
        nonlocal done
        while done < row // piece_rows:
            relay(done)
            done += 1

    def relay_next():
        nonlocal done
        if done < CHUNKS:
            relay(done)
            done += 1

    lax.fori_loop(0, 3, fill, 0)
    load_obs.wait()
    convert(obs, 0, 0, half)
    relay_next()
    convert(obs, 0, half, half)
    relay_next()
    load_omega.wait()
    weights(0)
    relay_next()
    products(0, 0, half)
    products(0, half, half)
    relay_next()
    relay_next()
    weights(1)
    relay_next()
    weights(2)
    for first, count in ((0, half), (half, half // 2), (half + half // 2, half // 2)):
        relay_to_row(first + count)
        convert(near, 1, first, count)
        relay_next()
        products(1, first, count)
        relay_next()
        for k in range(first // piece_rows, (first + count) // piece_rows):
            far_copies[k].wait_recv()
        convert(far, 2, first, count)
        relay_next()
        products(2, first, count)
    for copy in far_copies:
        copy.wait_send()

    for first in (0, half):
        rows = pl.ds(first, half)
        for start in range(0, TB, STEP):
            sums = []
            for b in range(start, start + STEP):
                total = cum[entry(0, kmax + b), rows, :]
                for kind in (1, 2):
                    total = total + cum[kind * (kmax + 1) + entry(kind, kmax + b), rows, :]
                sums.append(total)
            for i, total in enumerate(sums):
                high, low = split(total)
                rs[start + i, rows, :] = jnp.concatenate([high, low], axis=1)

    def forward(kind, slot):
        place = jnp.maximum(position(kind, slot), 0)
        both = jnp.dot(
            xt[kind * TB + lax.div(place, TB)], rs[lax.rem(place, TB)], preferred_element_type=f32
        )
        both = both[:BLK] + both[BLK:]
        return both[:, :BLK] + both[:, BLK:]

    def mate(slot):
        return slot + lax.div(slot, TB) * (1 - 2 * lax.rem(slot, 2))

    paired_here = share % 2 == 0
    parts = 2 if paired_here else 1
    size = share // parts

    def row_copy(kind, q, p):
        bit = q & -q
        part = pl.ds(p * size, size) if bit == nr // 2 else pl.ds(0, share)
        return pltpu.make_async_remote_copy(
            fbuf.at[kind, q, part], rbuf.at[kind, q - 1, part], row_send.at[kind, q - 1, p],
            row_recv.at[kind, q - 1, p], device_id={"row": flip(r, bit)}, device_id_type=MESH,
        )

    row_copies = {
        (kind, q, p): row_copy(kind, q, p)
        for kind in range(3)
        for q in range(1, nr)
        for p in range(parts if q == nr // 2 else 1)
    }

    def group(kind, q):
        first = flip(r, q) * share

        values = []
        for s in range(share):
            part = forward(kind, first + s)
            if kind == 0 and not paired_here:
                part = part + forward(kind, mate(first + s)).T
            values.append(part)
        for s, part in enumerate(values):
            fbuf[kind, q, s] = part

    def settle(kind, q):
        low = q & -q if q else nr // 2
        bit = 1
        while bit < low:
            row_copies[kind, q | bit, 0].wait_recv()
            fbuf[kind, q] = fbuf[kind, q] + rbuf[kind, (q | bit) - 1]
            bit *= 2
        if q:
            for p in range(parts if q == nr // 2 else 1):
                row_copies[kind, q, p].start()

    def add_last(kind, p):
        row_copies[kind, nr // 2, p].wait_recv()
        part = pl.ds(p * size, size)
        fbuf[kind, 0, part] = fbuf[kind, 0, part] + rbuf[kind, nr // 2 - 1, part]

    mirrors = {
        (kind, p): pltpu.make_async_remote_copy(
            fbuf.at[kind, 0, pl.ds(p * size, size)], mrecv.at[kind - 1, pl.ds(p * size, size)],
            mir_send.at[kind - 1, p], mir_recv.at[kind - 1, p],
            device_id={"col": near_col if kind == 1 else far_col}, device_id_type=MESH,
        )
        for kind in (1, 2)
        for p in range(parts)
    }

    def mirror(kind):
        for p in range(parts):
            add_last(kind, p)
            mirrors[kind, p].start()

    sent, kept = range(nr - 1, nr // 2 - 1, -1), range(nr // 2 - 1, -1, -1)
    order = [(2, q) for q in sent] + [(1, q) for q in sent] + [(2, q) for q in kept]
    order += [(0, q) for q in sent] + [(1, q) for q in kept] + [(0, q) for q in kept]
    waiting = []
    for item in order:
        group(*item)
        if item[1] % 2:
            settle(*item)
        for held in waiting:
            settle(*held)
        waiting = [] if item[1] % 2 else [item]
        if item == (1, 0):
            mirror(2)
    for held in waiting:
        settle(*held)
    mirror(1)
    scale = 0.5 / (samples * nr)
    eye = lax.broadcasted_iota(jnp.int32, (BLK, BLK), 0) == lax.broadcasted_iota(jnp.int32, (BLK, BLK), 1)

    def finish(kind, s, mirrored):
        slot = r * share + s
        place = position(kind, slot)
        gradient = fbuf[kind, 0, s] * scale if mirrored is None else (fbuf[kind, 0, s] + mirrored) * scale
        old = omega[0, strip[kind], slot]
        edge = step_size * penalty
        if kind == 0:
            on_diagonal = eye & (lax.div(place, TB) == lax.rem(place, TB)) & (place >= 0)
            inverse = jnp.where(on_diagonal, 1.0 / jnp.where(on_diagonal, old, 1.0), 0.0)
            gradient = gradient - inverse
        trial = old - step_size * gradient
        shrunk = jnp.where(trial > edge, trial - edge, jnp.where(trial < -edge, trial + edge, 0.0))
        if kind == 0:
            shrunk = jnp.where(on_diagonal, trial, shrunk)
        out[0, strip[kind], s] = jnp.where(place >= 0, shrunk, 0.0)

    def finish_outer(kind):
        for p in range(parts):
            mirrors[kind, p].wait_recv()
            for s in range(p * size, (p + 1) * size):
                finish(kind, s, mrecv[kind - 1, s].T)

    finish_outer(2)
    for p in range(parts):
        add_last(0, p)
    for s in range(share):
        if paired_here:
            other = s + lax.div(r * share, TB) * (1 - 2 * (s % 2))
            finish(0, s, fbuf[0, 0, other].T)
        else:
            finish(0, s, None)
    finish_outer(1)
    for copy in row_copies.values():
        copy.wait_send()
    for copy in mirrors.values():
        copy.wait_send()


def solution(mesh):
    nr, nc = mesh.shape["row"], mesh.shape["col"]

    def on_device(observations, omega, block_slots):
        samples, width = observations.shape
        kmax = omega.shape[2]
        share = kmax // nr
        parts = 2 if share % 2 == 0 else 1
        vmem, here = pl.BlockSpec(memory_space=pltpu.VMEM), pl.BlockSpec(memory_space=pl.ANY)
        dma = pltpu.SemaphoreType.DMA
        return pl.pallas_call(
            functools.partial(kernel, nr, nc, kmax),
            out_shape=jax.ShapeDtypeStruct((1, 3, share, BLK, BLK), f32),
            in_specs=[pl.BlockSpec(memory_space=pltpu.SMEM), here, here],
            out_specs=vmem,
            scratch_shapes=[
                pltpu.SMEM((3, kmax + TB), jnp.int32),
                pltpu.VMEM((samples, width), f32),
                pltpu.VMEM(omega.shape, f32),
                pltpu.VMEM((samples, width), f32),
                pltpu.VMEM((samples, width), f32),
                pltpu.VMEM((3 * TB, samples, 2 * BLK), bf16),
                pltpu.VMEM((3 * TB, 2 * BLK, samples), bf16),
                pltpu.VMEM((3 * kmax, 2 * BLK, 2 * BLK), bf16),
                pltpu.VMEM((3 * (kmax + 1), samples, BLK), f32),
                pltpu.VMEM((TB, samples, 2 * BLK), bf16),
                pltpu.VMEM((3, nr, share, BLK, BLK), f32),
                pltpu.VMEM((3, nr - 1, share, BLK, BLK), f32),
                pltpu.VMEM((2, share, BLK, BLK), f32),
                dma((2,)),
                dma((CHUNKS,)),
                dma((CHUNKS,)),
                dma((CHUNKS,)),
                dma((CHUNKS,)),
                dma((3, nr - 1, parts)),
                dma((3, nr - 1, parts)),
                dma((2, parts)),
                dma((2, parts)),
            ],
            compiler_params=pltpu.CompilerParams(
                collective_id=0, has_side_effects=True, vmem_limit_bytes=54400 * 1024
            ),
        )(jnp.transpose(block_slots, (1, 0, 2)), observations, omega)

    return jax.shard_map(
        on_device,
        mesh=mesh,
        in_specs=(P("row", "col"), P("col", None, None, None, None), P("col", None, None)),
        out_specs=P("col", None, "row", None, None),
        check_vma=False,
    )
```

```python
import functools

import jax
import jax.numpy as jnp
from jax import lax
from jax.experimental import pallas as pl
from jax.experimental.pallas import tpu as pltpu
from jax.sharding import PartitionSpec as P

MESH = pl.DeviceIdType.MESH
BLK = 128
TB = 8
CHUNKS = 16
STEP = 4
WINDOW = 4

step_size = 0.5
penalty = 0.1
f32, bf16 = jnp.float32, jnp.bfloat16


def split(value):
    high = value.astype(bf16)
    return high, (value - high.astype(f32)).astype(bf16)


def flip(index, mask):
    out, bit = index, 1
    while bit <= mask:
        if mask & bit:
            out = out + bit * (1 - 2 * lax.rem(lax.div(index, bit), 2))
        bit *= 2
    return out


def kernel(
    nr, nc, kmax, slots, obs_in, omega_in, out, tab, obs, omega, near, far, xs, xt, wcat, cum, rs, fbuf, rbuf,
    mrecv, load, near_send, near_recv, far_send, far_recv, row_send, row_recv, mir_send, mir_recv,
    pre, pre_send, pre_recv,
):
    samples = obs_in.shape[0]
    load_obs = pltpu.make_async_copy(obs_in, obs, load.at[0])
    load_omega = pltpu.make_async_copy(omega_in, omega, load.at[1])
    share = kmax // nr
    bits = nr.bit_length() - 1
    r, c = lax.axis_index("row"), lax.axis_index("col")
    odd = lax.rem(c, 2)
    near_col = c + 1 - 2 * odd
    far_col = lax.rem(c - 1 + 2 * odd + nc, nc)
    relay_to = lax.rem(c + 2 - 4 * odd + nc, nc)
    relay_from = lax.rem(c - 2 + 4 * odd + nc, nc)
    strip = (1, 2 - 2 * odd, 2 * odd)

    barrier = pltpu.get_barrier_semaphore()
    partners = [{"col": near_col}, {"col": far_col}, {"col": relay_from}]
    partners += [{"row": flip(r, 1 << k)} for k in range(bits)]
    for partner in partners:
        pl.semaphore_signal(barrier, inc=1, device_id=partner, device_id_type=MESH)
    load_obs.start()
    load_omega.start()
    pl.semaphore_wait(barrier, len(partners))

    piece = samples // CHUNKS

    def near_copy(k):
        rows = pl.ds(k * piece, piece)
        return pltpu.make_async_remote_copy(
            obs_in.at[rows], near.at[rows], near_send.at[k], near_recv.at[k],
            device_id={"col": near_col}, device_id_type=MESH,
        )

    def far_copy(k):
        rows = pl.ds(k * piece, piece)
        return pltpu.make_async_remote_copy(
            near.at[rows], far.at[rows], far_send.at[k], far_recv.at[k],
            device_id={"col": relay_to}, device_id_type=MESH,
        )

    near_copies = [near_copy(k) for k in range(CHUNKS)]
    far_copies = [far_copy(k) for k in range(CHUNKS)]
    for copy in near_copies[:WINDOW]:
        copy.start()

    def relay(k):
        near_copies[k].wait_recv()
        far_copies[k].start()
        near_copies[k].wait_send()
        if k + WINDOW < CHUNKS:
            near_copies[k + WINDOW].start()

    def convert(source, kind, first, count):
        rows = pl.ds(first, count)
        for a in range(TB):
            block = source[rows, pl.ds(a * BLK, BLK)]
            high, low = split(block)
            xs[kind * TB + a, rows, :] = jnp.concatenate([high, low], axis=1)
            high, low = split(block.T)
            xt[kind * TB + a, :, rows] = jnp.concatenate([high, low], axis=0)

    def fill(e, _):
        places = [slots[e, 0, j] for j in range(kmax)]
        columns = [jnp.where(p >= 0, lax.rem(jnp.maximum(p, 0), TB), TB) for p in places]
        for j in range(kmax):
            before = jnp.int32(kmax)
            for i in range(j):
                before = jnp.where(columns[i] == columns[j], i, before)
            tab[e, j] = before
        for b in range(TB):
            last = jnp.int32(kmax)
            for j in range(kmax):
                last = jnp.where(columns[j] == b, j, last)
            tab[e, kmax + b] = last
        return 0

    def entry(kind, at):
        return tab[strip[kind], at]

    def position(kind, slot):
        return slots[strip[kind], 0, slot]

    def weights(kind):
        def body(step, _):
            built = []
            for i in range(STEP):
                slot = step * STEP + i
                live = position(kind, slot) >= 0
                built.append(split(jnp.where(live, omega[0, strip[kind], slot], 0.0)))
            for i, (high, low) in enumerate(built):
                top = jnp.concatenate([high, low], axis=1)
                bottom = jnp.concatenate([high, jnp.zeros_like(low)], axis=1)
                wcat[kind * kmax + step * STEP + i] = jnp.concatenate([top, bottom], axis=0)
            return 0

        lax.fori_loop(0, kmax // STEP, body, 0)
        cum[kind * (kmax + 1) + kmax] = jnp.zeros((samples, BLK), f32)

    def products(kind, first, count):
        rows = pl.ds(first, count)

        def body(step, _):
            made = []
            for i in range(STEP):
                slot = step * STEP + i
                a = lax.div(jnp.maximum(position(kind, slot), 0), TB)
                both = jnp.dot(
                    xs[kind * TB + a, rows, :], wcat[kind * kmax + slot], preferred_element_type=f32
                )
                made.append(both[:, :BLK] + both[:, BLK:])
            for i, value in enumerate(made):
                slot = step * STEP + i
                before = cum[kind * (kmax + 1) + entry(kind, slot), rows, :]
                cum[kind * (kmax + 1) + slot, rows, :] = before + value
            return 0

        lax.fori_loop(0, kmax // STEP, body, 0, unroll=2)

    piece_rows = samples // CHUNKS
    half = samples // 2
    done = 0

    def relay_to_row(row):
        nonlocal done
        while done < row // piece_rows:
            relay(done)
            done += 1

    def relay_next():
        nonlocal done
        if done < CHUNKS:
            relay(done)
            done += 1

    lax.fori_loop(0, 3, fill, 0)
    load_obs.wait()
    convert(obs, 0, 0, half)
    relay_next()
    convert(obs, 0, half, half)
    relay_next()
    load_omega.wait()
    weights(0)
    relay_next()
    products(0, 0, half)
    products(0, half, half)
    relay_next()
    relay_next()
    weights(1)
    relay_next()
    weights(2)
    for first, count in ((0, half), (half, half // 2), (half + half // 2, half // 2)):
        relay_to_row(first + count)
        convert(near, 1, first, count)
        relay_next()
        products(1, first, count)
        relay_next()
        for k in range(first // piece_rows, (first + count) // piece_rows):
            far_copies[k].wait_recv()
        convert(far, 2, first, count)
        relay_next()
        products(2, first, count)
    for copy in far_copies:
        copy.wait_send()

    for first in (0, half):
        rows = pl.ds(first, half)
        for start in range(0, TB, STEP):
            sums = []
            for b in range(start, start + STEP):
                total = cum[entry(0, kmax + b), rows, :]
                for kind in (1, 2):
                    total = total + cum[kind * (kmax + 1) + entry(kind, kmax + b), rows, :]
                sums.append(total)
            for i, total in enumerate(sums):
                high, low = split(total)
                rs[start + i, rows, :] = jnp.concatenate([high, low], axis=1)

    def forward(kind, slot):
        place = jnp.maximum(position(kind, slot), 0)
        both = jnp.dot(
            xt[kind * TB + lax.div(place, TB)], rs[lax.rem(place, TB)], preferred_element_type=f32
        )
        both = both[:BLK] + both[BLK:]
        return both[:, :BLK] + both[:, BLK:]

    def mate(slot):
        return slot + lax.div(slot, TB) * (1 - 2 * lax.rem(slot, 2))

    paired_here = share % 2 == 0
    parts = 2 if paired_here else 1
    size = share // parts

    def row_copy(kind, q, p):
        bit = q & -q
        part = pl.ds(p * size, size) if bit == nr // 2 else pl.ds(0, share)
        if kind == 1 and q == nr // 2 and paired_here:
            part = pl.ds(odd * size, size)
        return pltpu.make_async_remote_copy(
            fbuf.at[kind, q, part], rbuf.at[kind, q - 1, part], row_send.at[kind, q - 1, p],
            row_recv.at[kind, q - 1, p], device_id={"row": flip(r, bit)}, device_id_type=MESH,
        )

    row_copies = {
        (kind, q, p): row_copy(kind, q, p)
        for kind in range(3)
        for q in range(1, nr)
        for p in range(parts if q == nr // 2 and not (kind == 1 and paired_here) else 1)
    }

    pre_copies = [
        pltpu.make_async_remote_copy(
            fbuf.at[1, q, pl.ds((1 - odd) * size, size)], pre.at[i], pre_send.at[i], pre_recv.at[i],
            device_id={"col": near_col}, device_id_type=MESH,
        )
        for i, q in enumerate((nr // 2, 0))
    ] if paired_here else []

    def add_pair(i, q):
        pre_copies[i].wait_recv()
        for s in range(size):
            at = odd * size + s
            fbuf[1, q, at] = fbuf[1, q, at] + pre[i, s].T

    def group(kind, q):
        first = flip(r, q) * share

        values = []
        for s in range(share):
            part = forward(kind, first + s)
            if kind == 0 and not paired_here:
                part = part + forward(kind, mate(first + s)).T
            values.append(part)
        for s, part in enumerate(values):
            fbuf[kind, q, s] = part

    def settle(kind, q):
        low = q & -q if q else nr // 2
        bit = 1
        while bit < low:
            row_copies[kind, q | bit, 0].wait_recv()
            fbuf[kind, q] = fbuf[kind, q] + rbuf[kind, (q | bit) - 1]
            bit *= 2
        if kind == 1 and paired_here and q in (0, nr // 2):
            pre_copies[0 if q else 1].start()
        elif q:
            for p in range(parts if q == nr // 2 else 1):
                row_copies[kind, q, p].start()

    def add_last(kind, p):
        row_copies[kind, nr // 2, p].wait_recv()
        part = pl.ds(p * size, size)
        fbuf[kind, 0, part] = fbuf[kind, 0, part] + rbuf[kind, nr // 2 - 1, part]

    mirrors = {
        (kind, p): pltpu.make_async_remote_copy(
            fbuf.at[kind, 0, pl.ds(p * size, size)], mrecv.at[kind - 1, pl.ds(p * size, size)],
            mir_send.at[kind - 1, p], mir_recv.at[kind - 1, p],
            device_id={"col": near_col if kind == 1 else far_col}, device_id_type=MESH,
        )
        for kind in ((2,) if paired_here else (1, 2))
        for p in range(parts)
    }

    def mirror(kind, p):
        add_last(kind, p)
        mirrors[kind, p].start()

    if paired_here:
        hand_back = pltpu.make_async_remote_copy(
            fbuf.at[1, 0, pl.ds(odd * size, size)], mrecv.at[0, pl.ds(odd * size, size)],
            mir_send.at[0, 0], mir_recv.at[0, 0], device_id={"col": near_col}, device_id_type=MESH,
        )

    sent, kept = range(nr - 1, nr // 2 - 1, -1), range(nr // 2 - 1, -1, -1)
    order = [(2, q) for q in sent] + [(1, q) for q in sent] + [(2, q) for q in kept]
    order += [(0, q) for q in sent] + [(1, q) for q in kept] + [(0, q) for q in kept]
    waiting = []
    for item in order:
        group(*item)
        if item[1] % 2:
            settle(*item)
        for held in waiting:
            settle(*held)
        waiting = [] if item[1] % 2 else [item]
        if item == (1, 0):
            mirror(2, 0)
        if item == (0, 1) and paired_here:
            add_pair(0, nr // 2)
            row_copies[1, nr // 2, 0].start()
    for p in range(1, parts):
        mirror(2, p)
    for held in waiting:
        settle(*held)
    if paired_here:
        add_pair(1, 0)
        row_copies[1, nr // 2, 0].wait_recv()
        mine = pl.ds(odd * size, size)
        fbuf[1, 0, mine] = fbuf[1, 0, mine] + rbuf[1, nr // 2 - 1, mine]
        hand_back.start()
    else:
        for p in range(parts):
            mirror(1, p)
    scale = 0.5 / (samples * nr)
    eye = lax.broadcasted_iota(jnp.int32, (BLK, BLK), 0) == lax.broadcasted_iota(jnp.int32, (BLK, BLK), 1)

    def finish(kind, s, mirrored, handed=False):
        slot = r * share + s
        place = position(kind, slot)
        gradient = mirrored * scale if handed else fbuf[kind, 0, s] * scale
        if mirrored is not None and not handed:
            gradient = (fbuf[kind, 0, s] + mirrored) * scale
        old = omega[0, strip[kind], slot]
        edge = step_size * penalty
        if kind == 0:
            on_diagonal = eye & (lax.div(place, TB) == lax.rem(place, TB)) & (place >= 0)
            inverse = jnp.where(on_diagonal, 1.0 / jnp.where(on_diagonal, old, 1.0), 0.0)
            gradient = gradient - inverse
        trial = old - step_size * gradient
        shrunk = jnp.where(trial > edge, trial - edge, jnp.where(trial < -edge, trial + edge, 0.0))
        if kind == 0:
            shrunk = jnp.where(on_diagonal, trial, shrunk)
        out[0, strip[kind], s] = jnp.where(place >= 0, shrunk, 0.0)

    def finish_outer(kind):
        for p in range(parts):
            mirrors[kind, p].wait_recv()
            for s in range(p * size, (p + 1) * size):
                finish(kind, s, mrecv[kind - 1, s].T)

    finish_outer(2)
    for p in range(parts):
        add_last(0, p)
    for s in range(share):
        if paired_here:
            other = s + lax.div(r * share, TB) * (1 - 2 * (s % 2))
            finish(0, s, fbuf[0, 0, other].T)
        else:
            finish(0, s, None)
    if paired_here:
        for s in range(size):
            finish(1, odd * size + s, None)
        hand_back.wait_recv()
        for s in range(size):
            at = (1 - odd) * size + s
            finish(1, at, mrecv[0, at].T, handed=True)
        for copy in (hand_back, *pre_copies):
            copy.wait_send()
    else:
        finish_outer(1)
    for copy in row_copies.values():
        copy.wait_send()
    for copy in mirrors.values():
        copy.wait_send()


def solution(mesh):
    nr, nc = mesh.shape["row"], mesh.shape["col"]

    def on_device(observations, omega, block_slots):
        samples, width = observations.shape
        kmax = omega.shape[2]
        share = kmax // nr
        parts = 2 if share % 2 == 0 else 1
        vmem, here = pl.BlockSpec(memory_space=pltpu.VMEM), pl.BlockSpec(memory_space=pl.ANY)
        dma = pltpu.SemaphoreType.DMA
        return pl.pallas_call(
            functools.partial(kernel, nr, nc, kmax),
            out_shape=jax.ShapeDtypeStruct((1, 3, share, BLK, BLK), f32),
            in_specs=[pl.BlockSpec(memory_space=pltpu.SMEM), here, here],
            out_specs=vmem,
            scratch_shapes=[
                pltpu.SMEM((3, kmax + TB), jnp.int32),
                pltpu.VMEM((samples, width), f32),
                pltpu.VMEM(omega.shape, f32),
                pltpu.VMEM((samples, width), f32),
                pltpu.VMEM((samples, width), f32),
                pltpu.VMEM((3 * TB, samples, 2 * BLK), bf16),
                pltpu.VMEM((3 * TB, 2 * BLK, samples), bf16),
                pltpu.VMEM((3 * kmax, 2 * BLK, 2 * BLK), bf16),
                pltpu.VMEM((3 * (kmax + 1), samples, BLK), f32),
                pltpu.VMEM((TB, samples, 2 * BLK), bf16),
                pltpu.VMEM((3, nr, share, BLK, BLK), f32),
                pltpu.VMEM((3, nr - 1, share, BLK, BLK), f32),
                pltpu.VMEM((2, share, BLK, BLK), f32),
                dma((2,)),
                dma((CHUNKS,)),
                dma((CHUNKS,)),
                dma((CHUNKS,)),
                dma((CHUNKS,)),
                dma((3, nr - 1, parts)),
                dma((3, nr - 1, parts)),
                dma((2, parts)),
                dma((2, parts)),
                pltpu.VMEM((2, max(share // 2, 1), BLK, BLK), f32),
                dma((2,)),
                dma((2,)),
            ],
            compiler_params=pltpu.CompilerParams(
                collective_id=0, has_side_effects=True, vmem_limit_bytes=54400 * 1024
            ),
        )(jnp.transpose(block_slots, (1, 0, 2)), observations, omega)

    return jax.shard_map(
        on_device,
        mesh=mesh,
        in_specs=(P("row", "col"), P("col", None, None, None, None), P("col", None, None)),
        out_specs=P("col", None, "row", None, None),
        check_vma=False,
    )
```

```python
import functools

import jax
import jax.numpy as jnp
from jax import lax
from jax.experimental import pallas as pl
from jax.experimental.pallas import tpu as pltpu
from jax.sharding import PartitionSpec as P

MESH = pl.DeviceIdType.MESH
BLK = 128
TB = 8
CHUNKS = 16
STEP = 4
WINDOW = 16

step_size = 0.5
penalty = 0.1
f32, bf16 = jnp.float32, jnp.bfloat16


def split(value):
    high = value.astype(bf16)
    return high, (value - high.astype(f32)).astype(bf16)


def flip(index, mask):
    out, bit = index, 1
    while bit <= mask:
        if mask & bit:
            out = out + bit * (1 - 2 * lax.rem(lax.div(index, bit), 2))
        bit *= 2
    return out


def kernel(
    nr, nc, kmax, slots, obs_in, omega_in, out, tab, obs, omega, near, far, xs, xt, wcat, cum, rs, fbuf, rbuf,
    mrecv, load, near_send, near_recv, far_send, far_recv, row_send, row_recv, mir_send, mir_recv,
    pre, pre_send, pre_recv,
):
    samples = obs_in.shape[0]
    load_obs = pltpu.make_async_copy(obs_in, obs, load.at[0])
    load_omega = pltpu.make_async_copy(omega_in, omega, load.at[1])
    share = kmax // nr
    bits = nr.bit_length() - 1
    r, c = lax.axis_index("row"), lax.axis_index("col")
    odd = lax.rem(c, 2)
    near_col = c + 1 - 2 * odd
    far_col = lax.rem(c - 1 + 2 * odd + nc, nc)
    relay_to = lax.rem(c + 2 - 4 * odd + nc, nc)
    relay_from = lax.rem(c - 2 + 4 * odd + nc, nc)
    strip = (1, 2 - 2 * odd, 2 * odd)

    barrier = pltpu.get_barrier_semaphore()
    partners = [{"col": near_col}, {"col": far_col}, {"col": relay_from}]
    partners += [{"row": flip(r, 1 << k)} for k in range(bits)]
    for partner in partners:
        pl.semaphore_signal(barrier, inc=1, device_id=partner, device_id_type=MESH)
    load_obs.start()
    load_omega.start()
    pl.semaphore_wait(barrier, len(partners))

    piece = samples // CHUNKS

    def near_copy(k):
        rows = pl.ds(k * piece, piece)
        return pltpu.make_async_remote_copy(
            obs_in.at[rows], near.at[rows], near_send.at[k], near_recv.at[k],
            device_id={"col": near_col}, device_id_type=MESH,
        )

    def far_copy(k):
        rows = pl.ds(k * piece, piece)
        return pltpu.make_async_remote_copy(
            near.at[rows], far.at[rows], far_send.at[k], far_recv.at[k],
            device_id={"col": relay_to}, device_id_type=MESH,
        )

    near_copies = [near_copy(k) for k in range(CHUNKS)]
    far_copies = [far_copy(k) for k in range(CHUNKS)]
    for copy in near_copies[:WINDOW]:
        copy.start()

    def relay(k):
        near_copies[k].wait_recv()
        far_copies[k].start()
        near_copies[k].wait_send()
        if k + WINDOW < CHUNKS:
            near_copies[k + WINDOW].start()

    def convert(source, kind, first, count):
        rows = pl.ds(first, count)
        for a in range(TB):
            block = source[rows, pl.ds(a * BLK, BLK)]
            high, low = split(block)
            xs[kind * TB + a, rows, :] = jnp.concatenate([high, low], axis=1)
            high, low = split(block.T)
            xt[kind * TB + a, :, rows] = jnp.concatenate([high, low], axis=0)

    def fill(e, _):
        places = [slots[e, 0, j] for j in range(kmax)]
        columns = [jnp.where(p >= 0, lax.rem(jnp.maximum(p, 0), TB), TB) for p in places]
        for j in range(kmax):
            before = jnp.int32(kmax)
            for i in range(j):
                before = jnp.where(columns[i] == columns[j], i, before)
            tab[e, j] = before
        for b in range(TB):
            last = jnp.int32(kmax)
            for j in range(kmax):
                last = jnp.where(columns[j] == b, j, last)
            tab[e, kmax + b] = last
        return 0

    def entry(kind, at):
        return tab[strip[kind], at]

    def position(kind, slot):
        return slots[strip[kind], 0, slot]

    def weights(kind):
        def body(step, _):
            built = []
            for i in range(STEP):
                slot = step * STEP + i
                live = position(kind, slot) >= 0
                built.append(split(jnp.where(live, omega[0, strip[kind], slot], 0.0)))
            for i, (high, low) in enumerate(built):
                top = jnp.concatenate([high, low], axis=1)
                bottom = jnp.concatenate([high, jnp.zeros_like(low)], axis=1)
                wcat[kind * kmax + step * STEP + i] = jnp.concatenate([top, bottom], axis=0)
            return 0

        lax.fori_loop(0, kmax // STEP, body, 0)
        cum[kind * (kmax + 1) + kmax] = jnp.zeros((samples, BLK), f32)

    def products(kind, first, count):
        rows = pl.ds(first, count)

        def body(step, _):
            made = []
            for i in range(STEP):
                slot = step * STEP + i
                a = lax.div(jnp.maximum(position(kind, slot), 0), TB)
                both = jnp.dot(
                    xs[kind * TB + a, rows, :], wcat[kind * kmax + slot], preferred_element_type=f32
                )
                made.append(both[:, :BLK] + both[:, BLK:])
            for i, value in enumerate(made):
                slot = step * STEP + i
                before = cum[kind * (kmax + 1) + entry(kind, slot), rows, :]
                cum[kind * (kmax + 1) + slot, rows, :] = before + value
            return 0

        lax.fori_loop(0, kmax // STEP, body, 0, unroll=2)

    piece_rows = samples // CHUNKS
    half = samples // 2
    done = 0

    def relay_to_row(row):
        nonlocal done
        while done < row // piece_rows:
            relay(done)
            done += 1

    def relay_next():
        nonlocal done
        if done < CHUNKS:
            relay(done)
            done += 1

    lax.fori_loop(0, 3, fill, 0)
    load_obs.wait()
    convert(obs, 0, 0, half)
    relay_next()
    convert(obs, 0, half, half)
    relay_next()
    load_omega.wait()
    weights(0)
    relay_next()
    products(0, 0, half)
    products(0, half, half)
    relay_next()
    relay_next()
    weights(1)
    relay_next()
    weights(2)
    for first, count in ((0, half), (half, half // 2), (half + half // 2, half // 2)):
        relay_to_row(first + count)
        convert(near, 1, first, count)
        relay_next()
        products(1, first, count)
        relay_next()
        for k in range(first // piece_rows, (first + count) // piece_rows):
            far_copies[k].wait_recv()
        convert(far, 2, first, count)
        relay_next()
        products(2, first, count)
    for copy in far_copies:
        copy.wait_send()

    for first in (0, half):
        rows = pl.ds(first, half)
        for start in range(0, TB, STEP):
            sums = []
            for b in range(start, start + STEP):
                total = cum[entry(0, kmax + b), rows, :]
                for kind in (1, 2):
                    total = total + cum[kind * (kmax + 1) + entry(kind, kmax + b), rows, :]
                sums.append(total)
            for i, total in enumerate(sums):
                high, low = split(total)
                rs[start + i, rows, :] = jnp.concatenate([high, low], axis=1)

    def forward(kind, slot):
        place = jnp.maximum(position(kind, slot), 0)
        both = jnp.dot(
            xt[kind * TB + lax.div(place, TB)], rs[lax.rem(place, TB)], preferred_element_type=f32
        )
        both = both[:BLK] + both[BLK:]
        return both[:, :BLK] + both[:, BLK:]

    def mate(slot):
        return slot + lax.div(slot, TB) * (1 - 2 * lax.rem(slot, 2))

    paired_here = share % 2 == 0
    parts = 2 if paired_here else 1
    size = share // parts

    def row_copy(kind, q, p):
        bit = q & -q
        part = pl.ds(p * size, size) if bit == nr // 2 else pl.ds(0, share)
        if kind == 1 and q == nr // 2 and paired_here:
            part = pl.ds(odd * size, size)
        return pltpu.make_async_remote_copy(
            fbuf.at[kind, q, part], rbuf.at[kind, q - 1, part], row_send.at[kind, q - 1, p],
            row_recv.at[kind, q - 1, p], device_id={"row": flip(r, bit)}, device_id_type=MESH,
        )

    row_copies = {
        (kind, q, p): row_copy(kind, q, p)
        for kind in range(3)
        for q in range(1, nr)
        for p in range(parts if q == nr // 2 and not (kind == 1 and paired_here) else 1)
    }

    pre_copies = [
        pltpu.make_async_remote_copy(
            fbuf.at[1, q, pl.ds((1 - odd) * size, size)], pre.at[i], pre_send.at[i], pre_recv.at[i],
            device_id={"col": near_col}, device_id_type=MESH,
        )
        for i, q in enumerate((nr // 2, 0))
    ] if paired_here else []

    def add_pair(i, q):
        pre_copies[i].wait_recv()
        for s in range(size):
            at = odd * size + s
            fbuf[1, q, at] = fbuf[1, q, at] + pre[i, s].T

    def group(kind, q):
        first = flip(r, q) * share

        values = []
        for s in range(share):
            part = forward(kind, first + s)
            if kind == 0 and not paired_here:
                part = part + forward(kind, mate(first + s)).T
            values.append(part)
        for s, part in enumerate(values):
            fbuf[kind, q, s] = part

    def settle(kind, q):
        low = q & -q if q else nr // 2
        bit = 1
        while bit < low:
            row_copies[kind, q | bit, 0].wait_recv()
            fbuf[kind, q] = fbuf[kind, q] + rbuf[kind, (q | bit) - 1]
            bit *= 2
        if kind == 1 and paired_here and q in (0, nr // 2):
            pre_copies[0 if q else 1].start()
        elif q:
            for p in range(parts if q == nr // 2 else 1):
                row_copies[kind, q, p].start()

    def add_last(kind, p):
        row_copies[kind, nr // 2, p].wait_recv()
        part = pl.ds(p * size, size)
        fbuf[kind, 0, part] = fbuf[kind, 0, part] + rbuf[kind, nr // 2 - 1, part]

    mirrors = {
        (kind, p): pltpu.make_async_remote_copy(
            fbuf.at[kind, 0, pl.ds(p * size, size)], mrecv.at[kind - 1, pl.ds(p * size, size)],
            mir_send.at[kind - 1, p], mir_recv.at[kind - 1, p],
            device_id={"col": near_col if kind == 1 else far_col}, device_id_type=MESH,
        )
        for kind in ((2,) if paired_here else (1, 2))
        for p in range(parts)
    }

    def mirror(kind, p):
        add_last(kind, p)
        mirrors[kind, p].start()

    if paired_here:
        hand_back = pltpu.make_async_remote_copy(
            fbuf.at[1, 0, pl.ds(odd * size, size)], mrecv.at[0, pl.ds(odd * size, size)],
            mir_send.at[0, 0], mir_recv.at[0, 0], device_id={"col": near_col}, device_id_type=MESH,
        )

    sent, kept = range(nr - 1, nr // 2 - 1, -1), range(nr // 2 - 1, -1, -1)
    order = [(2, q) for q in sent] + [(1, q) for q in sent] + [(2, q) for q in kept]
    order += [(0, q) for q in sent] + [(1, q) for q in kept] + [(0, q) for q in kept]
    waiting = []
    for item in order:
        group(*item)
        if item[1] % 2:
            settle(*item)
        for held in waiting:
            settle(*held)
        waiting = [] if item[1] % 2 else [item]
        if item == (1, 0):
            mirror(2, 0)
        if item == (0, 1) and paired_here:
            add_pair(0, nr // 2)
            row_copies[1, nr // 2, 0].start()
    for p in range(1, parts):
        mirror(2, p)
    for held in waiting:
        settle(*held)
    if paired_here:
        add_pair(1, 0)
        row_copies[1, nr // 2, 0].wait_recv()
        mine = pl.ds(odd * size, size)
        fbuf[1, 0, mine] = fbuf[1, 0, mine] + rbuf[1, nr // 2 - 1, mine]
        hand_back.start()
    else:
        for p in range(parts):
            mirror(1, p)
    scale = 0.5 / (samples * nr)
    eye = lax.broadcasted_iota(jnp.int32, (BLK, BLK), 0) == lax.broadcasted_iota(jnp.int32, (BLK, BLK), 1)

    def finish(kind, s, mirrored, handed=False):
        slot = r * share + s
        place = position(kind, slot)
        gradient = mirrored * scale if handed else fbuf[kind, 0, s] * scale
        if mirrored is not None and not handed:
            gradient = (fbuf[kind, 0, s] + mirrored) * scale
        old = omega[0, strip[kind], slot]
        edge = step_size * penalty
        if kind == 0:
            on_diagonal = eye & (lax.div(place, TB) == lax.rem(place, TB)) & (place >= 0)
            inverse = jnp.where(on_diagonal, 1.0 / jnp.where(on_diagonal, old, 1.0), 0.0)
            gradient = gradient - inverse
        trial = old - step_size * gradient
        shrunk = jnp.where(trial > edge, trial - edge, jnp.where(trial < -edge, trial + edge, 0.0))
        if kind == 0:
            shrunk = jnp.where(on_diagonal, trial, shrunk)
        out[0, strip[kind], s] = jnp.where(place >= 0, shrunk, 0.0)

    def finish_outer(kind):
        for p in range(parts):
            mirrors[kind, p].wait_recv()
            for s in range(p * size, (p + 1) * size):
                finish(kind, s, mrecv[kind - 1, s].T)

    finish_outer(2)
    for p in range(parts):
        add_last(0, p)
    for s in range(share):
        if paired_here:
            other = s + lax.div(r * share, TB) * (1 - 2 * (s % 2))
            finish(0, s, fbuf[0, 0, other].T)
        else:
            finish(0, s, None)
    if paired_here:
        for s in range(size):
            finish(1, odd * size + s, None)
        hand_back.wait_recv()
        for s in range(size):
            at = (1 - odd) * size + s
            finish(1, at, mrecv[0, at].T, handed=True)
        for copy in (hand_back, *pre_copies):
            copy.wait_send()
    else:
        finish_outer(1)
    for copy in row_copies.values():
        copy.wait_send()
    for copy in mirrors.values():
        copy.wait_send()


def solution(mesh):
    nr, nc = mesh.shape["row"], mesh.shape["col"]

    def on_device(observations, omega, block_slots):
        samples, width = observations.shape
        kmax = omega.shape[2]
        share = kmax // nr
        parts = 2 if share % 2 == 0 else 1
        vmem, here = pl.BlockSpec(memory_space=pltpu.VMEM), pl.BlockSpec(memory_space=pl.ANY)
        dma = pltpu.SemaphoreType.DMA
        return pl.pallas_call(
            functools.partial(kernel, nr, nc, kmax),
            out_shape=jax.ShapeDtypeStruct((1, 3, share, BLK, BLK), f32),
            in_specs=[pl.BlockSpec(memory_space=pltpu.SMEM), here, here],
            out_specs=vmem,
            scratch_shapes=[
                pltpu.SMEM((3, kmax + TB), jnp.int32),
                pltpu.VMEM((samples, width), f32),
                pltpu.VMEM(omega.shape, f32),
                pltpu.VMEM((samples, width), f32),
                pltpu.VMEM((samples, width), f32),
                pltpu.VMEM((3 * TB, samples, 2 * BLK), bf16),
                pltpu.VMEM((3 * TB, 2 * BLK, samples), bf16),
                pltpu.VMEM((3 * kmax, 2 * BLK, 2 * BLK), bf16),
                pltpu.VMEM((3 * (kmax + 1), samples, BLK), f32),
                pltpu.VMEM((TB, samples, 2 * BLK), bf16),
                pltpu.VMEM((3, nr, share, BLK, BLK), f32),
                pltpu.VMEM((3, nr - 1, share, BLK, BLK), f32),
                pltpu.VMEM((2, share, BLK, BLK), f32),
                dma((2,)),
                dma((CHUNKS,)),
                dma((CHUNKS,)),
                dma((CHUNKS,)),
                dma((CHUNKS,)),
                dma((3, nr - 1, parts)),
                dma((3, nr - 1, parts)),
                dma((2, parts)),
                dma((2, parts)),
                pltpu.VMEM((2, max(share // 2, 1), BLK, BLK), f32),
                dma((2,)),
                dma((2,)),
            ],
            compiler_params=pltpu.CompilerParams(
                collective_id=0, has_side_effects=True, vmem_limit_bytes=54400 * 1024
            ),
        )(jnp.transpose(block_slots, (1, 0, 2)), observations, omega)

    return jax.shard_map(
        on_device,
        mesh=mesh,
        in_specs=(P("row", "col"), P("col", None, None, None, None), P("col", None, None)),
        out_specs=P("col", None, "row", None, None),
        check_vma=False,
    )
```

```python
import functools

import jax
import jax.numpy as jnp
from jax import lax
from jax.experimental import pallas as pl
from jax.experimental.pallas import tpu as pltpu
from jax.sharding import PartitionSpec as P

MESH = pl.DeviceIdType.MESH
BLK = 128
TB = 8
CHUNKS = 16
STEP = 4
WINDOW = 16

step_size = 0.5
penalty = 0.1
f32, bf16 = jnp.float32, jnp.bfloat16


def split(value):
    high = value.astype(bf16)
    return high, (value - high.astype(f32)).astype(bf16)


def flip(index, mask):
    out, bit = index, 1
    while bit <= mask:
        if mask & bit:
            out = out + bit * (1 - 2 * lax.rem(lax.div(index, bit), 2))
        bit *= 2
    return out


def kernel(
    nr, nc, kmax, slots, obs_in, omega_in, out, tab, obs, omega, near, far, xs, xt, wcat, cum, rs, fbuf, rbuf,
    mrecv, load, near_send, near_recv, far_send, far_recv, row_send, row_recv, mir_send, mir_recv,
    pre, pre_send, pre_recv,
):
    samples = obs_in.shape[0]
    load_obs = pltpu.make_async_copy(obs_in, obs, load.at[0])
    load_omega = pltpu.make_async_copy(omega_in, omega, load.at[1])
    share = kmax // nr
    bits = nr.bit_length() - 1
    r, c = lax.axis_index("row"), lax.axis_index("col")
    odd = lax.rem(c, 2)
    near_col = c + 1 - 2 * odd
    far_col = lax.rem(c - 1 + 2 * odd + nc, nc)
    relay_to = lax.rem(c + 2 - 4 * odd + nc, nc)
    relay_from = lax.rem(c - 2 + 4 * odd + nc, nc)
    strip = (1, 2 - 2 * odd, 2 * odd)

    barrier = pltpu.get_barrier_semaphore()
    partners = [{"col": near_col}, {"col": far_col}, {"col": relay_from}]
    partners += [{"row": flip(r, 1 << k)} for k in range(bits)]
    for partner in partners:
        pl.semaphore_signal(barrier, inc=1, device_id=partner, device_id_type=MESH)
    load_obs.start()
    load_omega.start()
    pl.semaphore_wait(barrier, len(partners))

    piece = samples // CHUNKS

    def near_copy(k):
        rows = pl.ds(k * piece, piece)
        return pltpu.make_async_remote_copy(
            obs_in.at[rows], near.at[rows], near_send.at[k], near_recv.at[k],
            device_id={"col": near_col}, device_id_type=MESH,
        )

    def far_copy(k):
        rows = pl.ds(k * piece, piece)
        return pltpu.make_async_remote_copy(
            near.at[rows], far.at[rows], far_send.at[k], far_recv.at[k],
            device_id={"col": relay_to}, device_id_type=MESH,
        )

    near_copies = [near_copy(k) for k in range(CHUNKS)]
    far_copies = [far_copy(k) for k in range(CHUNKS)]
    for copy in near_copies[:WINDOW]:
        copy.start()

    def relay(k):
        near_copies[k].wait_recv()
        far_copies[k].start()
        near_copies[k].wait_send()
        if k + WINDOW < CHUNKS:
            near_copies[k + WINDOW].start()

    def convert(source, kind, first, count):
        rows = pl.ds(first, count)
        for a in range(TB):
            block = source[rows, pl.ds(a * BLK, BLK)]
            high, low = split(block)
            xs[kind * TB + a, rows, :] = jnp.concatenate([high, low], axis=1)
            high, low = split(block.T)
            xt[kind * TB + a, :, rows] = jnp.concatenate([high, low], axis=0)

    def fill(e, _):
        places = [slots[e, 0, j] for j in range(kmax)]
        columns = [jnp.where(p >= 0, lax.rem(jnp.maximum(p, 0), TB), TB) for p in places]
        for j in range(kmax):
            before = jnp.int32(kmax)
            for i in range(j):
                before = jnp.where(columns[i] == columns[j], i, before)
            tab[e, j] = before
        for b in range(TB):
            last = jnp.int32(kmax)
            for j in range(kmax):
                last = jnp.where(columns[j] == b, j, last)
            tab[e, kmax + b] = last
        return 0

    def entry(kind, at):
        return tab[strip[kind], at]

    def position(kind, slot):
        return slots[strip[kind], 0, slot]

    def weights(kind):
        def body(step, _):
            built = []
            for i in range(STEP):
                slot = step * STEP + i
                live = position(kind, slot) >= 0
                built.append(split(jnp.where(live, omega[0, strip[kind], slot], 0.0)))
            for i, (high, low) in enumerate(built):
                top = jnp.concatenate([high, low], axis=1)
                bottom = jnp.concatenate([high, jnp.zeros_like(low)], axis=1)
                wcat[kind * kmax + step * STEP + i] = jnp.concatenate([top, bottom], axis=0)
            return 0

        lax.fori_loop(0, kmax // STEP, body, 0)
        cum[kind * (kmax + 1) + kmax] = jnp.zeros((samples, BLK), f32)

    def products(kind, first, count):
        rows = pl.ds(first, count)

        def body(step, _):
            made = []
            for i in range(STEP):
                slot = step * STEP + i
                a = lax.div(jnp.maximum(position(kind, slot), 0), TB)
                both = jnp.dot(
                    xs[kind * TB + a, rows, :], wcat[kind * kmax + slot], preferred_element_type=f32
                )
                made.append(both[:, :BLK] + both[:, BLK:])
            for i, value in enumerate(made):
                slot = step * STEP + i
                before = cum[kind * (kmax + 1) + entry(kind, slot), rows, :]
                cum[kind * (kmax + 1) + slot, rows, :] = before + value
            return 0

        lax.fori_loop(0, kmax // STEP, body, 0, unroll=2)

    piece_rows = samples // CHUNKS
    half = samples // 2
    done = 0

    def relay_to_row(row):
        nonlocal done
        while done < row // piece_rows:
            relay(done)
            done += 1

    def relay_next():
        nonlocal done
        if done < CHUNKS:
            relay(done)
            done += 1

    lax.fori_loop(0, 3, fill, 0)
    load_obs.wait()
    convert(obs, 0, 0, half)
    relay_next()
    convert(obs, 0, half, half)
    relay_next()
    load_omega.wait()
    weights(0)
    relay_next()
    products(0, 0, half)
    products(0, half, half)
    relay_next()
    relay_next()
    weights(1)
    relay_next()
    weights(2)
    for first, count in ((0, half), (half, half // 2), (half + half // 2, half // 2)):
        relay_to_row(first + count)
        convert(near, 1, first, count)
        relay_next()
        products(1, first, count)
        relay_next()
        for k in range(first // piece_rows, (first + count) // piece_rows):
            far_copies[k].wait_recv()
        convert(far, 2, first, count)
        relay_next()
        products(2, first, count)
    for copy in far_copies:
        copy.wait_send()

    for first in (0, half):
        rows = pl.ds(first, half)
        for start in range(0, TB, STEP):
            sums = []
            for b in range(start, start + STEP):
                total = cum[entry(0, kmax + b), rows, :]
                for kind in (1, 2):
                    total = total + cum[kind * (kmax + 1) + entry(kind, kmax + b), rows, :]
                sums.append(total)
            for i, total in enumerate(sums):
                high, low = split(total)
                rs[start + i, rows, :] = jnp.concatenate([high, low], axis=1)

    def forward(kind, slot):
        place = jnp.maximum(position(kind, slot), 0)
        both = jnp.dot(
            xt[kind * TB + lax.div(place, TB)], rs[lax.rem(place, TB)], preferred_element_type=f32
        )
        both = both[:BLK] + both[BLK:]
        return both[:, :BLK] + both[:, BLK:]

    def mate(slot):
        return slot + lax.div(slot, TB) * (1 - 2 * lax.rem(slot, 2))

    paired_here = share % 2 == 0
    parts = 2 if paired_here else 1
    size = share // parts

    def row_copy(kind, q, p):
        bit = q & -q
        part = pl.ds(p * size, size) if bit == nr // 2 else pl.ds(0, share)
        if kind == 1 and q == nr // 2 and paired_here:
            part = pl.ds(odd * size, size)
        return pltpu.make_async_remote_copy(
            fbuf.at[kind, q, part], rbuf.at[kind, q - 1, part], row_send.at[kind, q - 1, p],
            row_recv.at[kind, q - 1, p], device_id={"row": flip(r, bit)}, device_id_type=MESH,
        )

    row_copies = {
        (kind, q, p): row_copy(kind, q, p)
        for kind in range(3)
        for q in range(1, nr)
        for p in range(parts if q == nr // 2 and not (kind == 1 and paired_here) else 1)
    }

    pre_copies = [
        pltpu.make_async_remote_copy(
            fbuf.at[1, q, pl.ds((1 - odd) * size, size)], pre.at[i], pre_send.at[i], pre_recv.at[i],
            device_id={"col": near_col}, device_id_type=MESH,
        )
        for i, q in enumerate((nr // 2, 0))
    ] if paired_here else []

    def add_pair(i, q):
        pre_copies[i].wait_recv()
        for s in range(size):
            at = odd * size + s
            fbuf[1, q, at] = fbuf[1, q, at] + pre[i, s].T

    def group(kind, q):
        first = flip(r, q) * share

        values = []
        for s in range(share):
            part = forward(kind, first + s)
            if kind == 0 and not paired_here:
                part = part + forward(kind, mate(first + s)).T
            values.append(part)
        for s, part in enumerate(values):
            fbuf[kind, q, s] = part

    def settle(kind, q):
        low = q & -q if q else nr // 2
        bit = 1
        while bit < low:
            row_copies[kind, q | bit, 0].wait_recv()
            fbuf[kind, q] = fbuf[kind, q] + rbuf[kind, (q | bit) - 1]
            bit *= 2
        if kind == 1 and paired_here and q in (0, nr // 2):
            pre_copies[0 if q else 1].start()
        elif q:
            for p in range(parts if q == nr // 2 else 1):
                row_copies[kind, q, p].start()

    def add_last(kind, p):
        row_copies[kind, nr // 2, p].wait_recv()
        part = pl.ds(p * size, size)
        fbuf[kind, 0, part] = fbuf[kind, 0, part] + rbuf[kind, nr // 2 - 1, part]

    mirrors = {
        (kind, p): pltpu.make_async_remote_copy(
            fbuf.at[kind, 0, pl.ds(p * size, size)], mrecv.at[kind - 1, pl.ds(p * size, size)],
            mir_send.at[kind - 1, p], mir_recv.at[kind - 1, p],
            device_id={"col": near_col if kind == 1 else far_col}, device_id_type=MESH,
        )
        for kind in ((2,) if paired_here else (1, 2))
        for p in range(parts)
    }

    def mirror(kind, p):
        add_last(kind, p)
        mirrors[kind, p].start()

    if paired_here:
        hand_back = pltpu.make_async_remote_copy(
            fbuf.at[1, 0, pl.ds(odd * size, size)], mrecv.at[0, pl.ds(odd * size, size)],
            mir_send.at[0, 0], mir_recv.at[0, 0], device_id={"col": near_col}, device_id_type=MESH,
        )

    sent, kept = range(nr - 1, nr // 2 - 1, -1), range(nr // 2 - 1, -1, -1)
    order = [(2, q) for q in sent] + [(1, q) for q in sent] + [(2, q) for q in kept]
    if paired_here:
        order += [(0, q) for q in sent[:-1]] + [(1, q) for q in kept[:-1]]
        order += [(0, nr // 2), (1, 0)] + [(0, q) for q in kept]
    else:
        order += [(0, q) for q in sent] + [(1, q) for q in kept] + [(0, q) for q in kept]
    waiting = []
    for item in order:
        if paired_here and item == (0, nr // 2):
            for held in waiting:
                settle(*held)
            waiting = []
            mirror(2, 0)
            add_pair(0, nr // 2)
            row_copies[1, nr // 2, 0].start()
        group(*item)
        at_once = item[1] % 2 or (paired_here and item == (0, nr // 2))
        if at_once:
            settle(*item)
        for held in waiting:
            settle(*held)
        waiting = [] if at_once else [item]
        if item == (1, 0) and not paired_here:
            mirror(2, 0)
    for p in range(1, parts):
        mirror(2, p)
    for held in waiting:
        settle(*held)
    if paired_here:
        add_pair(1, 0)
        row_copies[1, nr // 2, 0].wait_recv()
        mine = pl.ds(odd * size, size)
        fbuf[1, 0, mine] = fbuf[1, 0, mine] + rbuf[1, nr // 2 - 1, mine]
        hand_back.start()
    else:
        for p in range(parts):
            mirror(1, p)
    scale = 0.5 / (samples * nr)
    eye = lax.broadcasted_iota(jnp.int32, (BLK, BLK), 0) == lax.broadcasted_iota(jnp.int32, (BLK, BLK), 1)

    def finish(kind, s, mirrored, handed=False):
        slot = r * share + s
        place = position(kind, slot)
        gradient = mirrored * scale if handed else fbuf[kind, 0, s] * scale
        if mirrored is not None and not handed:
            gradient = (fbuf[kind, 0, s] + mirrored) * scale
        old = omega[0, strip[kind], slot]
        edge = step_size * penalty
        if kind == 0:
            on_diagonal = eye & (lax.div(place, TB) == lax.rem(place, TB)) & (place >= 0)
            inverse = jnp.where(on_diagonal, 1.0 / jnp.where(on_diagonal, old, 1.0), 0.0)
            gradient = gradient - inverse
        trial = old - step_size * gradient
        shrunk = jnp.where(trial > edge, trial - edge, jnp.where(trial < -edge, trial + edge, 0.0))
        if kind == 0:
            shrunk = jnp.where(on_diagonal, trial, shrunk)
        out[0, strip[kind], s] = jnp.where(place >= 0, shrunk, 0.0)

    def finish_outer(kind):
        for p in range(parts):
            mirrors[kind, p].wait_recv()
            for s in range(p * size, (p + 1) * size):
                finish(kind, s, mrecv[kind - 1, s].T)

    finish_outer(2)
    for p in range(parts):
        add_last(0, p)
    for s in range(share):
        if paired_here:
            other = s + lax.div(r * share, TB) * (1 - 2 * (s % 2))
            finish(0, s, fbuf[0, 0, other].T)
        else:
            finish(0, s, None)
    if paired_here:
        for s in range(size):
            finish(1, odd * size + s, None)
        hand_back.wait_recv()
        for s in range(size):
            at = (1 - odd) * size + s
            finish(1, at, mrecv[0, at].T, handed=True)
        for copy in (hand_back, *pre_copies):
            copy.wait_send()
    else:
        finish_outer(1)
    for copy in row_copies.values():
        copy.wait_send()
    for copy in mirrors.values():
        copy.wait_send()


def solution(mesh):
    nr, nc = mesh.shape["row"], mesh.shape["col"]

    def on_device(observations, omega, block_slots):
        samples, width = observations.shape
        kmax = omega.shape[2]
        share = kmax // nr
        parts = 2 if share % 2 == 0 else 1
        vmem, here = pl.BlockSpec(memory_space=pltpu.VMEM), pl.BlockSpec(memory_space=pl.ANY)
        dma = pltpu.SemaphoreType.DMA
        return pl.pallas_call(
            functools.partial(kernel, nr, nc, kmax),
            out_shape=jax.ShapeDtypeStruct((1, 3, share, BLK, BLK), f32),
            in_specs=[pl.BlockSpec(memory_space=pltpu.SMEM), here, here],
            out_specs=vmem,
            scratch_shapes=[
                pltpu.SMEM((3, kmax + TB), jnp.int32),
                pltpu.VMEM((samples, width), f32),
                pltpu.VMEM(omega.shape, f32),
                pltpu.VMEM((samples, width), f32),
                pltpu.VMEM((samples, width), f32),
                pltpu.VMEM((3 * TB, samples, 2 * BLK), bf16),
                pltpu.VMEM((3 * TB, 2 * BLK, samples), bf16),
                pltpu.VMEM((3 * kmax, 2 * BLK, 2 * BLK), bf16),
                pltpu.VMEM((3 * (kmax + 1), samples, BLK), f32),
                pltpu.VMEM((TB, samples, 2 * BLK), bf16),
                pltpu.VMEM((3, nr, share, BLK, BLK), f32),
                pltpu.VMEM((3, nr - 1, share, BLK, BLK), f32),
                pltpu.VMEM((2, share, BLK, BLK), f32),
                dma((2,)),
                dma((CHUNKS,)),
                dma((CHUNKS,)),
                dma((CHUNKS,)),
                dma((CHUNKS,)),
                dma((3, nr - 1, parts)),
                dma((3, nr - 1, parts)),
                dma((2, parts)),
                dma((2, parts)),
                pltpu.VMEM((2, max(share // 2, 1), BLK, BLK), f32),
                dma((2,)),
                dma((2,)),
            ],
            compiler_params=pltpu.CompilerParams(
                collective_id=0, has_side_effects=True, vmem_limit_bytes=54400 * 1024
            ),
        )(jnp.transpose(block_slots, (1, 0, 2)), observations, omega)

    return jax.shard_map(
        on_device,
        mesh=mesh,
        in_specs=(P("row", "col"), P("col", None, None, None, None), P("col", None, None)),
        out_specs=P("col", None, "row", None, None),
        check_vma=False,
    )
```

```python
import functools

import jax
import jax.numpy as jnp
from jax import lax
from jax.experimental import pallas as pl
from jax.experimental.pallas import tpu as pltpu
from jax.sharding import PartitionSpec as P

MESH = pl.DeviceIdType.MESH
BLK = 128
TB = 8
CHUNKS = 32
STEP = 4
WINDOW = 32

step_size = 0.5
penalty = 0.1
f32, bf16 = jnp.float32, jnp.bfloat16


def split(value):
    high = value.astype(bf16)
    return high, (value - high.astype(f32)).astype(bf16)


def flip(index, mask):
    out, bit = index, 1
    while bit <= mask:
        if mask & bit:
            out = out + bit * (1 - 2 * lax.rem(lax.div(index, bit), 2))
        bit *= 2
    return out


def kernel(
    nr, nc, kmax, slots, obs_in, omega_in, out, tab, obs, omega, near, far, xs, xt, wcat, cum, rs, fbuf, rbuf,
    mrecv, load, near_send, near_recv, far_send, far_recv, row_send, row_recv, mir_send, mir_recv,
):
    samples = obs_in.shape[0]
    load_obs = pltpu.make_async_copy(obs_in, obs, load.at[0])
    load_omega = pltpu.make_async_copy(omega_in, omega, load.at[1])
    share = kmax // nr
    bits = nr.bit_length() - 1
    r, c = lax.axis_index("row"), lax.axis_index("col")
    odd = lax.rem(c, 2)
    near_col = c + 1 - 2 * odd
    far_col = lax.rem(c - 1 + 2 * odd + nc, nc)
    relay_to = lax.rem(c + 2 - 4 * odd + nc, nc)
    relay_from = lax.rem(c - 2 + 4 * odd + nc, nc)
    strip = (1, 2 - 2 * odd, 2 * odd)

    barrier = pltpu.get_barrier_semaphore()
    partners = [{"col": near_col}, {"col": far_col}, {"col": relay_from}]
    partners += [{"row": flip(r, 1 << k)} for k in range(bits)]
    for partner in partners:
        pl.semaphore_signal(barrier, inc=1, device_id=partner, device_id_type=MESH)
    load_obs.start()
    load_omega.start()
    pl.semaphore_wait(barrier, len(partners))

    piece = samples // CHUNKS

    def near_copy(k):
        rows = pl.ds(k * piece, piece)
        return pltpu.make_async_remote_copy(
            obs_in.at[rows], near.at[rows], near_send.at[k], near_recv.at[k],
            device_id={"col": near_col}, device_id_type=MESH,
        )

    def far_copy(k):
        rows = pl.ds(k * piece, piece)
        return pltpu.make_async_remote_copy(
            near.at[rows], far.at[rows], far_send.at[k], far_recv.at[k],
            device_id={"col": relay_to}, device_id_type=MESH,
        )

    near_copies = [near_copy(k) for k in range(CHUNKS)]
    far_copies = [far_copy(k) for k in range(CHUNKS)]
    for copy in near_copies[:WINDOW]:
        copy.start()

    def relay(k):
        near_copies[k].wait_recv()
        far_copies[k].start()
        near_copies[k].wait_send()
        if k + WINDOW < CHUNKS:
            near_copies[k + WINDOW].start()

    def convert(source, kind, first, count):
        rows = pl.ds(first, count)
        for a in range(TB):
            block = source[rows, pl.ds(a * BLK, BLK)]
            high, low = split(block)
            xs[kind * TB + a, rows, :] = jnp.concatenate([high, low], axis=1)
            high, low = split(block.T)
            xt[kind * TB + a, :, rows] = jnp.concatenate([high, low], axis=0)

    def fill(e, _):
        places = [slots[e, 0, j] for j in range(kmax)]
        columns = [jnp.where(p >= 0, lax.rem(jnp.maximum(p, 0), TB), TB) for p in places]
        for j in range(kmax):
            before = jnp.int32(kmax)
            for i in range(j):
                before = jnp.where(columns[i] == columns[j], i, before)
            tab[e, j] = before
        for b in range(TB):
            last = jnp.int32(kmax)
            for j in range(kmax):
                last = jnp.where(columns[j] == b, j, last)
            tab[e, kmax + b] = last
        return 0

    def entry(kind, at):
        return tab[strip[kind], at]

    def position(kind, slot):
        return slots[strip[kind], 0, slot]

    def weights(kind):
        def body(step, _):
            built = []
            for i in range(STEP):
                slot = step * STEP + i
                live = position(kind, slot) >= 0
                built.append(split(jnp.where(live, omega[0, strip[kind], slot], 0.0)))
            for i, (high, low) in enumerate(built):
                top = jnp.concatenate([high, low], axis=1)
                bottom = jnp.concatenate([high, jnp.zeros_like(low)], axis=1)
                wcat[kind * kmax + step * STEP + i] = jnp.concatenate([top, bottom], axis=0)
            return 0

        lax.fori_loop(0, kmax // STEP, body, 0)
        cum[kind * (kmax + 1) + kmax] = jnp.zeros((samples, BLK), f32)

    def products(kind, first, count):
        rows = pl.ds(first, count)

        def body(step, _):
            made = []
            for i in range(STEP):
                slot = step * STEP + i
                a = lax.div(jnp.maximum(position(kind, slot), 0), TB)
                both = jnp.dot(
                    xs[kind * TB + a, rows, :], wcat[kind * kmax + slot], preferred_element_type=f32
                )
                made.append(both[:, :BLK] + both[:, BLK:])
            for i, value in enumerate(made):
                slot = step * STEP + i
                before = cum[kind * (kmax + 1) + entry(kind, slot), rows, :]
                cum[kind * (kmax + 1) + slot, rows, :] = before + value
            return 0

        lax.fori_loop(0, kmax // STEP, body, 0, unroll=2)

    piece_rows = samples // CHUNKS
    half = samples // 2
    done = 0

    def relay_to_row(row):
        nonlocal done
        while done < row // piece_rows:
            relay(done)
            done += 1

    def relay_next():
        nonlocal done
        for _ in range(2):
            if done < CHUNKS:
                relay(done)
                done += 1

    lax.fori_loop(0, 3, fill, 0)
    load_obs.wait()
    convert(obs, 0, 0, half)
    relay_next()
    convert(obs, 0, half, half)
    relay_next()
    load_omega.wait()
    weights(0)
    relay_next()
    products(0, 0, half)
    products(0, half, half)
    relay_next()
    relay_next()
    weights(1)
    relay_next()
    weights(2)
    for first, count in ((0, half), (half, half // 2), (half + half // 2, half // 2)):
        relay_to_row(first + count)
        convert(near, 1, first, count)
        relay_next()
        products(1, first, count)
        relay_next()
        for k in range(first // piece_rows, (first + count) // piece_rows):
            far_copies[k].wait_recv()
        convert(far, 2, first, count)
        relay_next()
        products(2, first, count)
    for copy in far_copies:
        copy.wait_send()

    for first in (0, half):
        rows = pl.ds(first, half)
        for start in range(0, TB, STEP):
            sums = []
            for b in range(start, start + STEP):
                total = cum[entry(0, kmax + b), rows, :]
                for kind in (1, 2):
                    total = total + cum[kind * (kmax + 1) + entry(kind, kmax + b), rows, :]
                sums.append(total)
            for i, total in enumerate(sums):
                high, low = split(total)
                rs[start + i, rows, :] = jnp.concatenate([high, low], axis=1)

    def forward(kind, slot):
        place = jnp.maximum(position(kind, slot), 0)
        both = jnp.dot(
            xt[kind * TB + lax.div(place, TB)], rs[lax.rem(place, TB)], preferred_element_type=f32
        )
        both = both[:BLK] + both[BLK:]
        return both[:, :BLK] + both[:, BLK:]

    def mate(slot):
        return slot + lax.div(slot, TB) * (1 - 2 * lax.rem(slot, 2))

    paired_here = share % 2 == 0
    parts = 2 if paired_here else 1
    size = share // parts

    def row_copy(kind, q, p):
        bit = q & -q
        part = pl.ds(p * size, size) if bit == nr // 2 else pl.ds(0, share)
        return pltpu.make_async_remote_copy(
            fbuf.at[kind, q, part], rbuf.at[kind, q - 1, part], row_send.at[kind, q - 1, p],
            row_recv.at[kind, q - 1, p], device_id={"row": flip(r, bit)}, device_id_type=MESH,
        )

    row_copies = {
        (kind, q, p): row_copy(kind, q, p)
        for kind in range(3)
        for q in range(1, nr)
        for p in range(parts if q == nr // 2 else 1)
    }

    def group(kind, q):
        first = flip(r, q) * share

        values = []
        for s in range(share):
            part = forward(kind, first + s)
            if kind == 0 and not paired_here:
                part = part + forward(kind, mate(first + s)).T
            values.append(part)
        for s, part in enumerate(values):
            fbuf[kind, q, s] = part

    def settle(kind, q):
        low = q & -q if q else nr // 2
        bit = 1
        while bit < low:
            row_copies[kind, q | bit, 0].wait_recv()
            fbuf[kind, q] = fbuf[kind, q] + rbuf[kind, (q | bit) - 1]
            bit *= 2
        if q:
            for p in range(parts if q == nr // 2 else 1):
                row_copies[kind, q, p].start()

    def add_last(kind, p):
        row_copies[kind, nr // 2, p].wait_recv()
        part = pl.ds(p * size, size)
        fbuf[kind, 0, part] = fbuf[kind, 0, part] + rbuf[kind, nr // 2 - 1, part]

    mirrors = {
        (kind, p): pltpu.make_async_remote_copy(
            fbuf.at[kind, 0, pl.ds(p * size, size)], mrecv.at[kind - 1, pl.ds(p * size, size)],
            mir_send.at[kind - 1, p], mir_recv.at[kind - 1, p],
            device_id={"col": near_col if kind == 1 else far_col}, device_id_type=MESH,
        )
        for kind in (1, 2)
        for p in range(parts)
    }

    def mirror(kind):
        for p in range(parts):
            add_last(kind, p)
            mirrors[kind, p].start()

    sent, kept = range(nr - 1, nr // 2 - 1, -1), range(nr // 2 - 1, -1, -1)
    order = [(2, q) for q in sent] + [(1, q) for q in sent] + [(2, q) for q in kept]
    order += [(0, q) for q in sent] + [(1, q) for q in kept] + [(0, q) for q in kept]
    waiting = []
    for item in order:
        group(*item)
        if item[1] % 2:
            settle(*item)
        for held in waiting:
            settle(*held)
        waiting = [] if item[1] % 2 else [item]
        if item == (1, 0):
            mirror(2)
    for held in waiting:
        settle(*held)
    mirror(1)
    scale = 0.5 / (samples * nr)
    eye = lax.broadcasted_iota(jnp.int32, (BLK, BLK), 0) == lax.broadcasted_iota(jnp.int32, (BLK, BLK), 1)

    def finish(kind, s, mirrored):
        slot = r * share + s
        place = position(kind, slot)
        gradient = fbuf[kind, 0, s] * scale if mirrored is None else (fbuf[kind, 0, s] + mirrored) * scale
        old = omega[0, strip[kind], slot]
        edge = step_size * penalty
        if kind == 0:
            on_diagonal = eye & (lax.div(place, TB) == lax.rem(place, TB)) & (place >= 0)
            inverse = jnp.where(on_diagonal, 1.0 / jnp.where(on_diagonal, old, 1.0), 0.0)
            gradient = gradient - inverse
        trial = old - step_size * gradient
        shrunk = jnp.where(trial > edge, trial - edge, jnp.where(trial < -edge, trial + edge, 0.0))
        if kind == 0:
            shrunk = jnp.where(on_diagonal, trial, shrunk)
        out[0, strip[kind], s] = jnp.where(place >= 0, shrunk, 0.0)

    def finish_outer(kind):
        for p in range(parts):
            mirrors[kind, p].wait_recv()
            for s in range(p * size, (p + 1) * size):
                finish(kind, s, mrecv[kind - 1, s].T)

    finish_outer(2)
    for p in range(parts):
        add_last(0, p)
    for s in range(share):
        if paired_here:
            other = s + lax.div(r * share, TB) * (1 - 2 * (s % 2))
            finish(0, s, fbuf[0, 0, other].T)
        else:
            finish(0, s, None)
    finish_outer(1)
    for copy in row_copies.values():
        copy.wait_send()
    for copy in mirrors.values():
        copy.wait_send()


def solution(mesh):
    nr, nc = mesh.shape["row"], mesh.shape["col"]

    def on_device(observations, omega, block_slots):
        samples, width = observations.shape
        kmax = omega.shape[2]
        share = kmax // nr
        parts = 2 if share % 2 == 0 else 1
        vmem, here = pl.BlockSpec(memory_space=pltpu.VMEM), pl.BlockSpec(memory_space=pl.ANY)
        dma = pltpu.SemaphoreType.DMA
        return pl.pallas_call(
            functools.partial(kernel, nr, nc, kmax),
            out_shape=jax.ShapeDtypeStruct((1, 3, share, BLK, BLK), f32),
            in_specs=[pl.BlockSpec(memory_space=pltpu.SMEM), here, here],
            out_specs=vmem,
            scratch_shapes=[
                pltpu.SMEM((3, kmax + TB), jnp.int32),
                pltpu.VMEM((samples, width), f32),
                pltpu.VMEM(omega.shape, f32),
                pltpu.VMEM((samples, width), f32),
                pltpu.VMEM((samples, width), f32),
                pltpu.VMEM((3 * TB, samples, 2 * BLK), bf16),
                pltpu.VMEM((3 * TB, 2 * BLK, samples), bf16),
                pltpu.VMEM((3 * kmax, 2 * BLK, 2 * BLK), bf16),
                pltpu.VMEM((3 * (kmax + 1), samples, BLK), f32),
                pltpu.VMEM((TB, samples, 2 * BLK), bf16),
                pltpu.VMEM((3, nr, share, BLK, BLK), f32),
                pltpu.VMEM((3, nr - 1, share, BLK, BLK), f32),
                pltpu.VMEM((2, share, BLK, BLK), f32),
                dma((2,)),
                dma((CHUNKS,)),
                dma((CHUNKS,)),
                dma((CHUNKS,)),
                dma((CHUNKS,)),
                dma((3, nr - 1, parts)),
                dma((3, nr - 1, parts)),
                dma((2, parts)),
                dma((2, parts)),
            ],
            compiler_params=pltpu.CompilerParams(
                collective_id=0, has_side_effects=True, vmem_limit_bytes=54400 * 1024
            ),
        )(jnp.transpose(block_slots, (1, 0, 2)), observations, omega)

    return jax.shard_map(
        on_device,
        mesh=mesh,
        in_specs=(P("row", "col"), P("col", None, None, None, None), P("col", None, None)),
        out_specs=P("col", None, "row", None, None),
        check_vma=False,
    )
```

```python
import functools

import jax
import jax.numpy as jnp
from jax import lax
from jax.experimental import pallas as pl
from jax.experimental.pallas import tpu as pltpu
from jax.sharding import PartitionSpec as P

MESH = pl.DeviceIdType.MESH
BLK = 128
TB = 8
CHUNKS = 16
STEP = 4
WINDOW = 16

step_size = 0.5
penalty = 0.1
f32, bf16 = jnp.float32, jnp.bfloat16


def split(value):
    high = value.astype(bf16)
    return high, (value - high.astype(f32)).astype(bf16)


def flip(index, mask):
    out, bit = index, 1
    while bit <= mask:
        if mask & bit:
            out = out + bit * (1 - 2 * lax.rem(lax.div(index, bit), 2))
        bit *= 2
    return out


def kernel(
    nr, nc, kmax, slots, obs_in, omega_in, out, tab, obs, omega, near, far, xs, xt, wcat, cum, rs, fbuf, rbuf,
    mrecv, load, near_send, near_recv, far_send, far_recv, row_send, row_recv, mir_send, mir_recv,
    pre, pre_send, pre_recv,
):
    samples = obs_in.shape[0]
    load_obs = pltpu.make_async_copy(obs_in, obs, load.at[0])
    load_omega = pltpu.make_async_copy(omega_in, omega, load.at[1])
    share = kmax // nr
    bits = nr.bit_length() - 1
    r, c = lax.axis_index("row"), lax.axis_index("col")
    odd = lax.rem(c, 2)
    near_col = c + 1 - 2 * odd
    far_col = lax.rem(c - 1 + 2 * odd + nc, nc)
    relay_to = lax.rem(c + 2 - 4 * odd + nc, nc)
    relay_from = lax.rem(c - 2 + 4 * odd + nc, nc)
    strip = (1, 2 - 2 * odd, 2 * odd)

    barrier = pltpu.get_barrier_semaphore()
    partners = [{"col": near_col}, {"col": far_col}, {"col": relay_from}]
    partners += [{"row": flip(r, 1 << k)} for k in range(bits)]
    for partner in partners:
        pl.semaphore_signal(barrier, inc=1, device_id=partner, device_id_type=MESH)
    load_obs.start()
    load_omega.start()
    pl.semaphore_wait(barrier, len(partners))

    piece = samples // CHUNKS

    def near_copy(k):
        rows = pl.ds(k * piece, piece)
        return pltpu.make_async_remote_copy(
            obs_in.at[rows], near.at[rows], near_send.at[k], near_recv.at[k],
            device_id={"col": near_col}, device_id_type=MESH,
        )

    def far_copy(k):
        rows = pl.ds(k * piece, piece)
        return pltpu.make_async_remote_copy(
            near.at[rows], far.at[rows], far_send.at[k], far_recv.at[k],
            device_id={"col": relay_to}, device_id_type=MESH,
        )

    near_copies = [near_copy(k) for k in range(CHUNKS)]
    far_copies = [far_copy(k) for k in range(CHUNKS)]
    for copy in near_copies[:WINDOW]:
        copy.start()

    def relay(k):
        near_copies[k].wait_recv()
        far_copies[k].start()
        near_copies[k].wait_send()
        if k + WINDOW < CHUNKS:
            near_copies[k + WINDOW].start()

    def convert(source, kind, first, count):
        rows = pl.ds(first, count)
        for a in range(TB):
            block = source[rows, pl.ds(a * BLK, BLK)]
            high, low = split(block)
            xs[kind * TB + a, rows, :] = jnp.concatenate([high, low], axis=1)
            high, low = split(block.T)
            xt[kind * TB + a, :, rows] = jnp.concatenate([high, low], axis=0)

    def fill(e, _):
        places = [slots[e, 0, j] for j in range(kmax)]
        columns = [jnp.where(p >= 0, lax.rem(jnp.maximum(p, 0), TB), TB) for p in places]
        for j in range(kmax):
            before = jnp.int32(kmax)
            for i in range(j):
                before = jnp.where(columns[i] == columns[j], i, before)
            tab[e, j] = before
        for b in range(TB):
            last = jnp.int32(kmax)
            for j in range(kmax):
                last = jnp.where(columns[j] == b, j, last)
            tab[e, kmax + b] = last
        return 0

    def entry(kind, at):
        return tab[strip[kind], at]

    def position(kind, slot):
        return slots[strip[kind], 0, slot]

    def weights(kind):
        def body(step, _):
            built = []
            for i in range(STEP):
                slot = step * STEP + i
                live = position(kind, slot) >= 0
                built.append(split(jnp.where(live, omega[0, strip[kind], slot], 0.0)))
            for i, (high, low) in enumerate(built):
                top = jnp.concatenate([high, low], axis=1)
                bottom = jnp.concatenate([high, jnp.zeros_like(low)], axis=1)
                wcat[kind * kmax + step * STEP + i] = jnp.concatenate([top, bottom], axis=0)
            return 0

        lax.fori_loop(0, kmax // STEP, body, 0)
        cum[kind * (kmax + 1) + kmax] = jnp.zeros((samples, BLK), f32)

    def products(kind, first, count):
        rows = pl.ds(first, count)

        def body(step, _):
            made = []
            for i in range(STEP):
                slot = step * STEP + i
                a = lax.div(jnp.maximum(position(kind, slot), 0), TB)
                both = jnp.dot(
                    xs[kind * TB + a, rows, :], wcat[kind * kmax + slot], preferred_element_type=f32
                )
                made.append(both[:, :BLK] + both[:, BLK:])
            for i, value in enumerate(made):
                slot = step * STEP + i
                before = cum[kind * (kmax + 1) + entry(kind, slot), rows, :]
                cum[kind * (kmax + 1) + slot, rows, :] = before + value
            return 0

        lax.fori_loop(0, kmax // STEP, body, 0, unroll=2)

    piece_rows = samples // CHUNKS
    half = samples // 2
    done = 0

    def relay_to_row(row):
        nonlocal done
        while done < row // piece_rows:
            relay(done)
            done += 1

    def relay_next():
        nonlocal done
        if done < CHUNKS:
            relay(done)
            done += 1

    lax.fori_loop(0, 3, fill, 0)
    load_obs.wait()
    convert(obs, 0, 0, half)
    relay_next()
    convert(obs, 0, half, half)
    relay_next()
    load_omega.wait()
    weights(0)
    relay_next()
    products(0, 0, half)
    products(0, half, half)
    relay_next()
    relay_next()
    weights(1)
    relay_next()
    weights(2)
    for first, count in ((0, half), (half, half)):
        relay_to_row(first + count)
        convert(near, 1, first, count)
        relay_next()
        products(1, first, count)
        relay_next()
        for k in range(first // piece_rows, (first + count) // piece_rows):
            far_copies[k].wait_recv()
        convert(far, 2, first, count)
        relay_next()
        products(2, first, count)
    for copy in far_copies:
        copy.wait_send()

    for first in (0, half):
        rows = pl.ds(first, half)
        for start in range(0, TB, STEP):
            sums = []
            for b in range(start, start + STEP):
                total = cum[entry(0, kmax + b), rows, :]
                for kind in (1, 2):
                    total = total + cum[kind * (kmax + 1) + entry(kind, kmax + b), rows, :]
                sums.append(total)
            for i, total in enumerate(sums):
                high, low = split(total)
                rs[start + i, rows, :] = jnp.concatenate([high, low], axis=1)

    def forward(kind, slot):
        place = jnp.maximum(position(kind, slot), 0)
        both = jnp.dot(
            xt[kind * TB + lax.div(place, TB)], rs[lax.rem(place, TB)], preferred_element_type=f32
        )
        both = both[:BLK] + both[BLK:]
        return both[:, :BLK] + both[:, BLK:]

    def mate(slot):
        return slot + lax.div(slot, TB) * (1 - 2 * lax.rem(slot, 2))

    paired_here = share % 2 == 0
    parts = 2 if paired_here else 1
    size = share // parts

    def row_copy(kind, q, p):
        bit = q & -q
        part = pl.ds(p * size, size) if bit == nr // 2 else pl.ds(0, share)
        if kind == 1 and q == nr // 2 and paired_here:
            part = pl.ds(odd * size, size)
        return pltpu.make_async_remote_copy(
            fbuf.at[kind, q, part], rbuf.at[kind, q - 1, part], row_send.at[kind, q - 1, p],
            row_recv.at[kind, q - 1, p], device_id={"row": flip(r, bit)}, device_id_type=MESH,
        )

    row_copies = {
        (kind, q, p): row_copy(kind, q, p)
        for kind in range(3)
        for q in range(1, nr)
        for p in range(parts if q == nr // 2 and not (kind == 1 and paired_here) else 1)
    }

    pre_copies = [
        pltpu.make_async_remote_copy(
            fbuf.at[1, q, pl.ds((1 - odd) * size, size)], pre.at[i], pre_send.at[i], pre_recv.at[i],
            device_id={"col": near_col}, device_id_type=MESH,
        )
        for i, q in enumerate((nr // 2, 0))
    ] if paired_here else []

    def add_pair(i, q):
        pre_copies[i].wait_recv()
        for s in range(size):
            at = odd * size + s
            fbuf[1, q, at] = fbuf[1, q, at] + pre[i, s].T

    def group(kind, q):
        first = flip(r, q) * share

        values = []
        for s in range(share):
            part = forward(kind, first + s)
            if kind == 0 and not paired_here:
                part = part + forward(kind, mate(first + s)).T
            values.append(part)
        for s, part in enumerate(values):
            fbuf[kind, q, s] = part

    def settle(kind, q):
        low = q & -q if q else nr // 2
        bit = 1
        while bit < low:
            row_copies[kind, q | bit, 0].wait_recv()
            fbuf[kind, q] = fbuf[kind, q] + rbuf[kind, (q | bit) - 1]
            bit *= 2
        if kind == 1 and paired_here and q in (0, nr // 2):
            pre_copies[0 if q else 1].start()
        elif q:
            for p in range(parts if q == nr // 2 else 1):
                row_copies[kind, q, p].start()

    def add_last(kind, p):
        row_copies[kind, nr // 2, p].wait_recv()
        part = pl.ds(p * size, size)
        fbuf[kind, 0, part] = fbuf[kind, 0, part] + rbuf[kind, nr // 2 - 1, part]

    mirrors = {
        (kind, p): pltpu.make_async_remote_copy(
            fbuf.at[kind, 0, pl.ds(p * size, size)], mrecv.at[kind - 1, pl.ds(p * size, size)],
            mir_send.at[kind - 1, p], mir_recv.at[kind - 1, p],
            device_id={"col": near_col if kind == 1 else far_col}, device_id_type=MESH,
        )
        for kind in ((2,) if paired_here else (1, 2))
        for p in range(parts)
    }

    def mirror(kind, p):
        add_last(kind, p)
        mirrors[kind, p].start()

    if paired_here:
        hand_back = pltpu.make_async_remote_copy(
            fbuf.at[1, 0, pl.ds(odd * size, size)], mrecv.at[0, pl.ds(odd * size, size)],
            mir_send.at[0, 0], mir_recv.at[0, 0], device_id={"col": near_col}, device_id_type=MESH,
        )

    sent, kept = range(nr - 1, nr // 2 - 1, -1), range(nr // 2 - 1, -1, -1)
    order = [(2, q) for q in sent] + [(1, q) for q in sent] + [(2, q) for q in kept]
    order += [(0, q) for q in sent] + [(1, q) for q in kept] + [(0, q) for q in kept]
    waiting = []
    for item in order:
        group(*item)
        if item[1] % 2:
            settle(*item)
        for held in waiting:
            settle(*held)
        waiting = [] if item[1] % 2 else [item]
        if item == (1, 0):
            mirror(2, 0)
        if item == (0, 1) and paired_here:
            add_pair(0, nr // 2)
            row_copies[1, nr // 2, 0].start()
    for p in range(1, parts):
        mirror(2, p)
    for held in waiting:
        settle(*held)
    if paired_here:
        add_pair(1, 0)
        row_copies[1, nr // 2, 0].wait_recv()
        mine = pl.ds(odd * size, size)
        fbuf[1, 0, mine] = fbuf[1, 0, mine] + rbuf[1, nr // 2 - 1, mine]
        hand_back.start()
    else:
        for p in range(parts):
            mirror(1, p)
    scale = 0.5 / (samples * nr)
    eye = lax.broadcasted_iota(jnp.int32, (BLK, BLK), 0) == lax.broadcasted_iota(jnp.int32, (BLK, BLK), 1)

    def finish(kind, s, mirrored, handed=False):
        slot = r * share + s
        place = position(kind, slot)
        gradient = mirrored * scale if handed else fbuf[kind, 0, s] * scale
        if mirrored is not None and not handed:
            gradient = (fbuf[kind, 0, s] + mirrored) * scale
        old = omega[0, strip[kind], slot]
        edge = step_size * penalty
        if kind == 0:
            on_diagonal = eye & (lax.div(place, TB) == lax.rem(place, TB)) & (place >= 0)
            inverse = jnp.where(on_diagonal, 1.0 / jnp.where(on_diagonal, old, 1.0), 0.0)
            gradient = gradient - inverse
        trial = old - step_size * gradient
        shrunk = jnp.where(trial > edge, trial - edge, jnp.where(trial < -edge, trial + edge, 0.0))
        if kind == 0:
            shrunk = jnp.where(on_diagonal, trial, shrunk)
        out[0, strip[kind], s] = jnp.where(place >= 0, shrunk, 0.0)

    def finish_outer(kind):
        for p in range(parts):
            mirrors[kind, p].wait_recv()
            for s in range(p * size, (p + 1) * size):
                finish(kind, s, mrecv[kind - 1, s].T)

    finish_outer(2)
    for p in range(parts):
        add_last(0, p)
    for s in range(share):
        if paired_here:
            other = s + lax.div(r * share, TB) * (1 - 2 * (s % 2))
            finish(0, s, fbuf[0, 0, other].T)
        else:
            finish(0, s, None)
    if paired_here:
        for s in range(size):
            finish(1, odd * size + s, None)
        hand_back.wait_recv()
        for s in range(size):
            at = (1 - odd) * size + s
            finish(1, at, mrecv[0, at].T, handed=True)
        for copy in (hand_back, *pre_copies):
            copy.wait_send()
    else:
        finish_outer(1)
    for copy in row_copies.values():
        copy.wait_send()
    for copy in mirrors.values():
        copy.wait_send()


def solution(mesh):
    nr, nc = mesh.shape["row"], mesh.shape["col"]

    def on_device(observations, omega, block_slots):
        samples, width = observations.shape
        kmax = omega.shape[2]
        share = kmax // nr
        parts = 2 if share % 2 == 0 else 1
        vmem, here = pl.BlockSpec(memory_space=pltpu.VMEM), pl.BlockSpec(memory_space=pl.ANY)
        dma = pltpu.SemaphoreType.DMA
        return pl.pallas_call(
            functools.partial(kernel, nr, nc, kmax),
            out_shape=jax.ShapeDtypeStruct((1, 3, share, BLK, BLK), f32),
            in_specs=[pl.BlockSpec(memory_space=pltpu.SMEM), here, here],
            out_specs=vmem,
            scratch_shapes=[
                pltpu.SMEM((3, kmax + TB), jnp.int32),
                pltpu.VMEM((samples, width), f32),
                pltpu.VMEM(omega.shape, f32),
                pltpu.VMEM((samples, width), f32),
                pltpu.VMEM((samples, width), f32),
                pltpu.VMEM((3 * TB, samples, 2 * BLK), bf16),
                pltpu.VMEM((3 * TB, 2 * BLK, samples), bf16),
                pltpu.VMEM((3 * kmax, 2 * BLK, 2 * BLK), bf16),
                pltpu.VMEM((3 * (kmax + 1), samples, BLK), f32),
                pltpu.VMEM((TB, samples, 2 * BLK), bf16),
                pltpu.VMEM((3, nr, share, BLK, BLK), f32),
                pltpu.VMEM((3, nr - 1, share, BLK, BLK), f32),
                pltpu.VMEM((2, share, BLK, BLK), f32),
                dma((2,)),
                dma((CHUNKS,)),
                dma((CHUNKS,)),
                dma((CHUNKS,)),
                dma((CHUNKS,)),
                dma((3, nr - 1, parts)),
                dma((3, nr - 1, parts)),
                dma((2, parts)),
                dma((2, parts)),
                pltpu.VMEM((2, max(share // 2, 1), BLK, BLK), f32),
                dma((2,)),
                dma((2,)),
            ],
            compiler_params=pltpu.CompilerParams(
                collective_id=0, has_side_effects=True, vmem_limit_bytes=54400 * 1024
            ),
        )(jnp.transpose(block_slots, (1, 0, 2)), observations, omega)

    return jax.shard_map(
        on_device,
        mesh=mesh,
        in_specs=(P("row", "col"), P("col", None, None, None, None), P("col", None, None)),
        out_specs=P("col", None, "row", None, None),
        check_vma=False,
    )
```
